128 devices in a mesh: fsdp: 16 (over x, z_hi, core), tp: 8 (over z_lo, y).
Axes of the slice: x: 4, y: 4, z: 4 (z_hi: 2, z_lo: 2; z = z_hi * 2 + z_lo), core: 2. Of those that a mesh axis runs over, the one named last changes fastest.
Arguments:
- hidden_activations_saved: bfloat16 [2048, 26624], P('fsdp', 'tp'), may hold values from -6 to 6
- output_cotangent: bfloat16 [2048, 16384], P('tp', 'fsdp'), may hold values from -6 to 6
- frozen_down_matrix: bfloat16 [26624, 16384], P('tp', 'fsdp'), may hold values from -0.0390625 to 0.0390625
- adapter_input_maps: bfloat16 [16, 26624, 16], P('fsdp', 'tp'), may hold values from -0.078125 to 0.078125
- adapter_output_maps: bfloat16 [16, 16, 16384], P('fsdp'), may hold values from -0.046875 to 0.046875
- block_tenant_ids: int32 [16], replicated, may hold values from 0 to 15
- block_token_rows: int32 [16], replicated, may hold values from 1 to 128
- tenant_storage_slot: int32 [16], replicated, may hold values from 0 to 15, each once
Outputs:
- hidden_gradient: bfloat16 [2048, 26624], P('fsdp', 'tp')
- grad_a: float32 [16, 26624, 16], P('fsdp', 'tp')
- output_map_gradient: float32 [16, 16, 16384], P('fsdp')
The draws below stay inside these ranges and needn't reach their ends.
Inputs may be any that keep to these rules, and one draw needn't show every extreme that they name: `tenant_storage_slot`: each slot number appears once.
All inputs are finite; a program needn't handle non-finite values.
Results may differ from the reference program's by a relative error of at most 0.0017.
Values may be sent and summed in bfloat16 or wider, within the bound.
A program may use at most 192 MiB of HBM per device.

```python
import math
import jax
import jax.numpy as jnp
import numpy as np
from jax import lax

MODEL_WIDTH = 16384
HIDDEN_WIDTH = 26624
ADAPTER_RANK = 16
BLOCK = 128
TOKEN_COUNT = 2048
BLOCKS = 16
TENANT_COUNT = 16


def set_ends(drawn, own_key, least, top_value):
    longest = drawn.shape.index(max(drawn.shape))
    spots = []
    for shift in (0, 1):
        where = [jax.random.randint(jax.random.fold_in(own_key, axis), (), 0, length) for axis, length in enumerate(drawn.shape)]
        where[longest] = (where[longest] + shift) % drawn.shape[longest]
        spots.append(tuple(where))
    return drawn.at[spots[0]].set(least).at[spots[1]].set(top_value)


def steps_of(stream_key, shape, cuts, smallest, high):
    loudness = 1.0
    for dim, blocks in cuts:
        steps = jax.random.uniform(jax.random.fold_in(jax.random.fold_in(stream_key, 6), dim), (blocks,), jnp.float32, smallest / len(cuts), high / len(cuts))
        loudness = loudness * jnp.repeat(jnp.exp(steps), shape[dim] // blocks).reshape((-1,) + (1,) * (len(shape) - 1 - dim))
    return loudness


def rank_table(count, skew):
    loads = [(1 << 20) // math.isqrt(grade ** skew) + 1 for grade in range(1, count + 1)]
    deviation = 1 + sum(loads) // (1 << 30)
    return np.cumsum(np.array([max(1, weight // deviation) for weight in loads]))


def ranked(rng, dims, number_of, slope):
    grid = rank_table(number_of, slope)
    lot = jax.random.randint(jax.random.fold_in(rng, 1), dims, 0, int(grid[number_of - 1]))
    grade = jnp.searchsorted(jnp.asarray(grid, jnp.int32), lot, side="right")
    return jax.random.permutation(jax.random.fold_in(rng, 2), number_of)[grade].astype(jnp.int32)


def bell_draw(key, dims, scale, most, pieces=(), kind=jnp.bfloat16):
    gain = steps_of(key, dims, pieces, -0.22, 0.18) if pieces else 1.0
    values = jax.random.normal(key, dims, jnp.float32) * scale * gain
    return jnp.minimum(jnp.maximum(values, -most), most).astype(kind)


def setup_inputs(seed: int = 0) -> dict:
    streams_of = jax.random.split(jax.random.key(seed), 9)
    return {
        "hidden_activations_saved": bell_draw(streams_of[0], (TOKEN_COUNT, HIDDEN_WIDTH), 1.0, 6.0, ((0, 16), (1, 8))),
        "output_cotangent": bell_draw(streams_of[1], (TOKEN_COUNT, MODEL_WIDTH), 1.0, 6.0, ((0, 8), (1, 16))),
        "frozen_down_matrix": bell_draw(streams_of[2], (HIDDEN_WIDTH, MODEL_WIDTH), HIDDEN_WIDTH ** -0.5, 0.0390625, ((0, 8), (1, 16))),
        "adapter_input_maps": bell_draw(streams_of[3], (TENANT_COUNT, HIDDEN_WIDTH, ADAPTER_RANK), (HIDDEN_WIDTH // 4) ** -0.5, 0.078125, ((0, 16), (1, 8))),
        "adapter_output_maps": bell_draw(streams_of[4], (TENANT_COUNT, ADAPTER_RANK, MODEL_WIDTH), MODEL_WIDTH ** -0.5, 0.046875, ((0, 16),)),
        "block_tenant_ids": set_ends(ranked(streams_of[5], (BLOCKS,), TENANT_COUNT, 2), jax.random.fold_in(streams_of[5], 3), 0, TENANT_COUNT - 1).astype(jnp.int32),
        "block_token_rows": set_ends(jax.random.randint(streams_of[6], (BLOCKS,), 1, BLOCK + 1), jax.random.fold_in(streams_of[6], 1), 1, BLOCK).astype(jnp.int32),
        "tenant_storage_slot": jax.random.permutation(streams_of[7], TENANT_COUNT).astype(jnp.int32),
    }


adapter_scale = 2.0


def reference(hidden_activations_saved, output_cotangent, frozen_down_matrix, adapter_input_maps, adapter_output_maps, block_tenant_ids, block_token_rows, tenant_storage_slot):
    current_block_slot = tenant_storage_slot[block_tenant_ids].astype(jnp.int32)
    live_rows = (jnp.arange(BLOCK, dtype=jnp.int32)[None, :] < block_token_rows[:, None]).reshape(TOKEN_COUNT)
    masked = jnp.where(live_rows[:, None], output_cotangent, jnp.zeros((), output_cotangent.dtype))
    masked_cotangent_float = masked.astype(jnp.float32).reshape(BLOCKS, BLOCK, MODEL_WIDTH)
    hidden_wide_float = hidden_activations_saved.astype(jnp.float32).reshape(BLOCKS, BLOCK, HIDDEN_WIDTH)
    output_map_current = adapter_output_maps[current_block_slot].astype(jnp.float32)
    input_map_current = adapter_input_maps[current_block_slot].astype(jnp.float32)
    reduced_output = (adapter_scale * jnp.einsum("uop,uqp->uoq", masked_cotangent_float, output_map_current)).astype(jnp.bfloat16)
    reduced_input = (adapter_scale * jnp.einsum("dju,dux->djx", hidden_wide_float, input_map_current)).astype(jnp.bfloat16)
    reduced_output_float = reduced_output.astype(jnp.float32)
    grad_a = jax.ops.segment_sum(jnp.einsum("bkf,bkr->bfr", hidden_wide_float, reduced_output_float), current_block_slot, num_segments=TENANT_COUNT)
    output_map_gradient = jax.ops.segment_sum(jnp.einsum("cyx,cym->cxm", reduced_input.astype(jnp.float32), masked_cotangent_float), current_block_slot, num_segments=TENANT_COUNT)
    frozen_gradient_part = lax.dot_general(masked, frozen_down_matrix, (((1,), (1,)), ((), ())), preferred_element_type=jnp.float32)
    adapter_gradient_part = jnp.einsum("pvq,ptq->pvt", reduced_output_float, input_map_current).reshape(TOKEN_COUNT, HIDDEN_WIDTH)
    hidden_gradient = (frozen_gradient_part + adapter_gradient_part).astype(jnp.bfloat16)
    return hidden_gradient, grad_a, output_map_gradient
```

```python
import functools
import math

import jax
import jax.numpy as jnp
from jax import lax
from jax.experimental import pallas as pl
from jax.experimental.pallas import tpu as pltpu
from jax.sharding import PartitionSpec as P

BLOCK = 128
TILE = 256
MESH = pl.DeviceIdType.MESH
adapter_scale = 2.0
f32 = jnp.float32
bf16 = jnp.bfloat16

TOP = 32000.0
STEPS = 8.0 / math.log(2.0)


def nt(a, b):
    return lax.dot_general(a, b, (((1,), (1,)), ((), ())), preferred_element_type=f32)


def nn(a, b):
    return lax.dot_general(a, b, (((1,), (0,)), ((), ())), preferred_element_type=f32)


def level_of(peak):
    return jnp.ceil(jnp.log(jnp.maximum(peak, 1e-30)) * STEPS)


def kernel(
    ids, live, store, h_ref, g_ref, w_ref, a_ref, b_ref,
    o_h, o_a, o_b,
    w_all, dy, stage, part, acc, out_q, in_q, a_all, b_all, a_sel,
    lin_part, lin_own, lin_all, low_part, low_in_parts, slot_terms, slot_other,
    da_own, da_all, da_send, da_other, spread,
    w_sem, gs, gr, ss, sr, vs, vr,
):
    fs = lax.axis_index("fsdp")
    t = lax.axis_index("tp")
    k, c = fs // 2, fs % 2
    y, zl = t % 4, t // 4
    hid = h_ref.shape[1]
    feat = g_ref.shape[1]
    rank = a_ref.shape[0]
    tiles = hid // TILE
    chips = 8

    def across(j):
        return {"fsdp": 2 * j + c, "tp": t}

    def along(tt):
        return {"fsdp": fs, "tp": tt}

    sibling = {"fsdp": 2 * k + 1 - c, "tp": t}

    def slot(b):
        return store[ids[b]]

    def place(s):
        return (s % 2) * chips + s // 2

    def send(src, dst, s_sem, r_sem, dev):
        return pltpu.make_async_remote_copy(
            src_ref=src, dst_ref=dst, send_sem=s_sem, recv_sem=r_sem,
            device_id=dev, device_id_type=MESH,
        )

    def others(me, body):
        def step(i, _):
            body(lax.rem(me + i, chips))
            return 0

        lax.fori_loop(1, chips, step, 0)

    barrier = pltpu.get_barrier_semaphore()
    pl.semaphore_signal(barrier, inc=1, device_id=sibling, device_id_type=MESH)
    others(k, lambda j: pl.semaphore_signal(barrier, inc=1, device_id=across(j), device_id_type=MESH))
    others(t, lambda j: pl.semaphore_signal(barrier, inc=1, device_id=along(j), device_id_type=MESH))

    mine = pl.ds(pl.multiple_of(c * feat, feat), feat)
    w_here = pltpu.make_async_copy(w_ref, w_all.at[:, mine], w_sem)
    w_here.start()

    def masked(j):
        rows = lax.broadcasted_iota(jnp.int32, (BLOCK, feat), 0)
        g = g_ref[pl.ds(pl.multiple_of(j * BLOCK, BLOCK), BLOCK), :]
        return jnp.where(rows < live[2 * t + j], g, jnp.zeros((), bf16))

    dy[y, zl, :, mine] = masked(c)
    stage[...] = masked(1 - c)
    pl.semaphore_wait(barrier, 15)

    to_sib = send(stage, dy.at[y, zl, :, mine], ss.at[0], sr.at[0], sibling)
    to_sib.start()
    w_out = send(w_ref, w_all.at[:, mine], ss.at[1], sr.at[1], sibling)
    w_out.start()
    to_sib.wait_recv()

    def dy_send(y_from, z_from, n, tt):
        at = z_from * 4 + y_from
        return send(dy.at[y_from, z_from], dy.at[y_from, z_from], gs.at[0, n], gr.at[0, at], along(tt))

    y_next, y_prev, y_far = lax.rem(y + 1, 4), lax.rem(y + 3, 4), lax.rem(y + 2, 4)
    own = [dy_send(y, zl, 0, (1 - zl) * 4 + y)]
    own += [dy_send(y, zl, 1 + i, zl * 4 + yy) for i, yy in enumerate((y_next, y_prev, y_far))]
    for cp in own:
        cp.start()

    def a_copy(j):
        return send(a_ref, a_all.at[c * chips + k], gs.at[1, j], gr.at[1, k], across(j))

    def b_copy(j):
        cols = pl.ds(pl.multiple_of(j * 2 * feat, 2 * feat), 2 * feat)
        return send(b_ref.at[:, cols], b_all.at[c * chips + k], gs.at[2, j], gr.at[2, k], across(j))

    others(k, lambda j: a_copy(j).start())
    others(k, lambda j: b_copy(j).start())
    a_all[c * chips + k] = a_ref[...]
    b_all[c * chips + k] = b_ref[:, pl.ds(pl.multiple_of(k * 2 * feat, 2 * feat), 2 * feat)]

    def dy_wait(yy, zz):
        at = zz * 4 + yy
        send(dy.at[yy, zz], dy.at[yy, zz], gs.at[0, 0], gr.at[0, at], sibling).wait_recv()

    dy_wait(y, 1 - zl)
    relay = [dy_send(y, 1 - zl, 4 + i, zl * 4 + yy) for i, yy in enumerate((y_next, y_prev, y_far))]
    for cp in relay:
        cp.start()

    def q_copy(j):
        return send(out_q.at[j], in_q.at[k], gs.at[3, j], gr.at[3, k], across(j))

    def main_step(yy):
        def tile(n, peak):
            at = pl.ds(pl.multiple_of(n * TILE, TILE), TILE)
            p = nt(dy[yy].reshape(2 * BLOCK, 2 * feat), w_all[at, :])
            part[:, at] = p
            p = jnp.abs(p)
            return jnp.maximum(peak, jnp.maximum(p[:, :128], p[:, 128:]))

        peak = lax.fori_loop(0, tiles, tile, jnp.zeros((2 * BLOCK, 128), f32))
        level = level_of(jnp.max(peak, axis=1, keepdims=True))
        gain = TOP * jnp.exp(level * (-1.0 / STEPS))
        for zz in range(2):
            j = zz * 4 + yy
            lo = zz * BLOCK

            @pl.when(j == k)
            def _():
                acc[...] = part[lo : lo + BLOCK, :]

            @pl.when(j != k)
            def _():
                def code(n, _):
                    at = pl.ds(pl.multiple_of(n * TILE, TILE), TILE)
                    q = jnp.round(part[lo : lo + BLOCK, at] * gain[lo : lo + BLOCK])
                    out_q[j, :, at] = q.astype(jnp.int32).astype(jnp.int16)
                    return 0

                lax.fori_loop(0, tiles, code, 0)
                marks = jnp.broadcast_to(level[lo : lo + BLOCK], (BLOCK, 128))
                out_q[j, :, hid:] = marks.astype(jnp.int32).astype(jnp.int16)
                q_copy(j).start()

    w_out.wait_recv()
    w_here.wait()
    main_step(y)

    others(k, lambda j: send(a_ref, a_all.at[c * chips + j], gs.at[1, j], gr.at[1, j], across(j)).wait_recv())
    others(k, lambda j: send(b_ref.at[:, : 2 * feat], b_all.at[c * chips + j], gs.at[2, j], gr.at[2, j], across(j)).wait_recv())
    half = pl.ds(c * chips, chips)
    a_fwd = send(a_all.at[half], a_all.at[half], ss.at[2], sr.at[2], sibling)
    b_fwd = send(b_all.at[half], b_all.at[half], ss.at[3], sr.at[3], sibling)
    a_fwd.start()
    b_fwd.start()
    a_fwd.wait_recv()
    a_sel[...] = a_all[place(slot(fs))]
    lin_part[t] = nt(a_sel[...], h_ref[...])

    def lin_copy(j):
        return send(lin_part.at[t], lin_part.at[t], gs.at[4, j], gr.at[4, t], along(j))

    others(t, lambda j: lin_copy(j).start())

    for zz in range(2):
        dy_wait(y_next, zz)
    main_step(y_next)

    others(t, lambda j: send(lin_part.at[j], lin_part.at[j], gs.at[4, j], gr.at[4, j], along(j)).wait_recv())
    total = lin_part[0]
    for j in range(1, chips):
        total = total + lin_part[j]
    lin_own[...] = (adapter_scale * total).astype(bf16)

    def lin_all_copy(j):
        return send(lin_own, lin_all.at[k], gs.at[5, j], gr.at[5, k], across(j))

    others(k, lambda j: lin_all_copy(j).start())
    lin_all[k] = lin_own[...]

    for zz in range(2):
        dy_wait(y_prev, zz)
    main_step(y_prev)
    for zz in range(2):
        dy_wait(y_far, zz)
    main_step(y_far)

    b_fwd.wait_recv()

    def low_step(j, _):
        low_part[j] = nt(b_all[place(slot(2 * j + c))], dy[j % 4, j // 4])
        return 0

    lax.fori_loop(0, chips, low_step, 0)

    def low_copy(j):
        return send(low_part.at[j], low_in_parts.at[k], gs.at[6, j], gr.at[6, k], across(j))

    others(k, lambda j: low_copy(j).start())
    low_in_parts[k] = low_part[k]

    others(k, lambda j: send(lin_own, lin_all.at[j], gs.at[5, j], gr.at[5, j], across(j)).wait_recv())
    for j in range(chips):
        at = ((j % 4) * 2 + j // 4) * BLOCK
        s = slot(2 * j + c)
        value = lin_all[j]
        for n in range(2 * chips):
            hit = (s == 2 * (n % chips) + n // chips).astype(f32).astype(bf16)
            spread[n * rank : (n + 1) * rank, at : at + BLOCK] = value * hit

    def slot_tile(n, _):
        at = pl.ds(pl.multiple_of(n * TILE, TILE), TILE)
        p = nn(spread[...], dy[:, :, :, at].reshape(chips * BLOCK, TILE))
        slot_terms[:, :, :, at] = p.reshape(2, chips, rank, TILE)
        return 0

    lax.fori_loop(0, 2 * feat // TILE, slot_tile, 0)
    slot_swap = send(slot_terms.at[1 - c], slot_other, ss.at[4], sr.at[4], sibling)
    slot_swap.start()

    others(k, lambda j: send(low_part.at[j], low_in_parts.at[j], gs.at[6, j], gr.at[6, j], across(j)).wait_recv())
    total = low_in_parts[0]
    for j in range(1, chips):
        total = total + low_in_parts[j]
    low = (adapter_scale * total).astype(bf16)
    da = nn(low, h_ref[...])
    level = level_of(jnp.max(jnp.abs(da), axis=1, keepdims=True))
    gain = TOP * jnp.exp(level * (-1.0 / STEPS))
    da_own[:, :hid] = jnp.round(da * gain).astype(jnp.int32).astype(jnp.int16)
    da_own[:, hid:] = jnp.broadcast_to(level, (rank, 128)).astype(jnp.int32).astype(jnp.int16)

    def da_copy(j):
        return send(da_own, da_all.at[k], gs.at[7, j], gr.at[7, k], across(j))

    others(k, lambda j: da_copy(j).start())
    da_all[k] = da_own[...]

    slot_swap.wait_recv()
    slot_terms[c] = slot_terms[c] + slot_other[...]

    def b_cols(j):
        return pl.ds(pl.multiple_of(j * 2 * feat, 2 * feat), 2 * feat)

    def ob_copy(j):
        return send(slot_terms.at[c, j], o_b.at[:, b_cols(k)], gs.at[8, j], gr.at[8, k], across(j))

    others(k, lambda j: ob_copy(j).start())
    o_b[:, b_cols(k)] = slot_terms[c, k]

    def add_part(j):
        send(out_q.at[j], in_q.at[j], gs.at[3, j], gr.at[3, j], across(j)).wait_recv()
        scale = jnp.exp(in_q[j, :, hid:].astype(f32) * (1.0 / STEPS)) * (1.0 / TOP)
        scale = jnp.concatenate([scale, scale], axis=1)

        def tile(n, _):
            at = pl.ds(pl.multiple_of(n * TILE, TILE), TILE)
            acc[:, at] += in_q[j, :, at].astype(f32) * scale
            return 0

        lax.fori_loop(0, tiles, tile, 0)

    others(k, add_part)
    low_rows = low.astype(f32).T.astype(bf16)

    def finish(n, _):
        at = pl.ds(pl.multiple_of(n * TILE, TILE), TILE)
        o_h[:, at] = (acc[:, at] + nn(low_rows, a_sel[:, at])).astype(bf16)
        return 0

    lax.fori_loop(0, tiles, finish, 0)

    others(k, lambda j: send(da_own, da_all.at[j], gs.at[7, j], gr.at[7, j], across(j)).wait_recv())

    def da_sum(s):
        out = jnp.zeros((rank, hid), f32)
        for j in range(chips):
            hit = (slot(2 * j + c) == s).astype(f32) * (1.0 / TOP)
            scale = jnp.exp(da_all[j, :, hid:].astype(f32) * (1.0 / STEPS))[:, :1] * hit
            out = out + da_all[j, :, :hid].astype(f32) * scale
        return out

    da_send[...] = da_sum(2 * k + 1 - c)
    da_swap = send(da_send, da_other, ss.at[5], sr.at[5], sibling)
    da_swap.start()
    o_a[...] = da_sum(2 * k + c)
    da_swap.wait_recv()
    o_a[...] += da_other[...]

    others(k, lambda j: send(slot_terms.at[c, j], o_b.at[:, b_cols(j)], gs.at[8, j], gr.at[8, j], across(j)).wait_recv())

    for cp in (to_sib, w_out, a_fwd, b_fwd, slot_swap, da_swap):
        cp.wait_send()
    for cp in own + relay:
        cp.wait_send()
    for copy in (a_copy, b_copy, q_copy, lin_all_copy, low_copy, da_copy, ob_copy):
        others(k, lambda j: copy(j).wait_send())
    others(t, lambda j: lin_copy(j).wait_send())


def local(h, g, w, a, b, ids, live, store):
    tok, hid = h.shape
    feat = g.shape[1]
    rank = a.shape[2]
    wide = b.shape[2]
    chips = 8
    a_t = jnp.swapaxes(a, 1, 2).reshape(rank, hid)
    vm = pl.BlockSpec(memory_space=pltpu.VMEM)
    sm = pl.BlockSpec(memory_space=pltpu.SMEM)
    dma = pltpu.SemaphoreType.DMA
    o_h, o_a, o_b = pl.pallas_call(
        kernel,
        out_shape=(
            jax.ShapeDtypeStruct((tok, hid), bf16),
            jax.ShapeDtypeStruct((rank, hid), f32),
            jax.ShapeDtypeStruct((rank, wide), f32),
        ),
        in_specs=[sm, sm, sm, vm, vm, pl.BlockSpec(memory_space=pl.ANY), vm, vm],
        out_specs=(vm, vm, vm),
        scratch_shapes=[
            pltpu.VMEM((hid, 2 * feat), bf16),
            pltpu.VMEM((4, 2, BLOCK, 2 * feat), bf16),
            pltpu.VMEM((BLOCK, feat), bf16),
            pltpu.VMEM((2 * BLOCK, hid), f32),
            pltpu.VMEM((BLOCK, hid), f32),
            pltpu.VMEM((chips, BLOCK, hid + 128), jnp.int16),
            pltpu.VMEM((chips, BLOCK, hid + 128), jnp.int16),
            pltpu.VMEM((2 * chips, rank, hid), bf16),
            pltpu.VMEM((2 * chips, rank, 2 * feat), bf16),
            pltpu.VMEM((rank, hid), bf16),
            pltpu.VMEM((chips, rank, BLOCK), f32),
            pltpu.VMEM((rank, BLOCK), bf16),
            pltpu.VMEM((chips, rank, BLOCK), bf16),
            pltpu.VMEM((chips, rank, BLOCK), f32),
            pltpu.VMEM((chips, rank, BLOCK), f32),
            pltpu.VMEM((2, chips, rank, 2 * feat), f32),
            pltpu.VMEM((chips, rank, 2 * feat), f32),
            pltpu.VMEM((rank, hid + 128), jnp.int16),
            pltpu.VMEM((chips, rank, hid + 128), jnp.int16),
            pltpu.VMEM((rank, hid), f32),
            pltpu.VMEM((rank, hid), f32),
            pltpu.VMEM((2 * chips * rank, chips * BLOCK), bf16),
            dma,
            dma((9, 8)),
            dma((9, 8)),
            dma((6,)),
            dma((6,)),
            dma((1,)),
            dma((1,)),
        ],
        compiler_params=pltpu.CompilerParams(
            collective_id=0, has_side_effects=True, vmem_limit_bytes=62 << 20
        ),
    )(ids, live, store, h, g, w, a_t, b.reshape(rank, wide))
    return (
        o_h,
        jnp.swapaxes(o_a.reshape(1, rank, hid), 1, 2),
        o_b.reshape(1, rank, wide),
    )


def solution(mesh):
    placed = (
        P("fsdp", "tp"),
        P("tp", "fsdp"),
        P("tp", "fsdp"),
        P("fsdp", "tp", None),
        P("fsdp", None, None),
        P(),
        P(),
        P(),
    )
    return jax.shard_map(
        local,
        mesh=mesh,
        in_specs=placed,
        out_specs=(P("fsdp", "tp"), P("fsdp", "tp", None), P("fsdp", None, None)),
        check_vma=False,
    )
```

```python
import functools
import math

import jax
import jax.numpy as jnp
from jax import lax
from jax.experimental import pallas as pl
from jax.experimental.pallas import tpu as pltpu
from jax.sharding import PartitionSpec as P

BLOCK = 128
TILE = 256
MESH = pl.DeviceIdType.MESH
adapter_scale = 2.0
f32 = jnp.float32
bf16 = jnp.bfloat16

TOP = 32000.0
STEPS = 8.0 / math.log(2.0)


def nt(a, b):
    return lax.dot_general(a, b, (((1,), (1,)), ((), ())), preferred_element_type=f32)


def nn(a, b):
    return lax.dot_general(a, b, (((1,), (0,)), ((), ())), preferred_element_type=f32)


def level_of(peak):
    return jnp.ceil(jnp.log(jnp.maximum(peak, 1e-30)) * STEPS)


def kernel(
    ids, live, store, h_ref, g_ref, w_ref, a_ref, b_ref,
    o_h, o_a, o_b,
    w_all, dy, stage, part, acc, out0, out1, out2, in0, in1, in2, a_all, b_all, a_sel,
    lin_part, lin_own, lin_all, low_part, low_in_parts, slot_terms, slot_other, slot_all,
    da_own, da_all, da_send, da_other, low_kept, spread,
    gs, gr, qs, qr, ws, wr, wl, ss, sr,
):
    fs = lax.axis_index("fsdp")
    t = lax.axis_index("tp")
    k, c = fs // 2, fs % 2
    x, zh = k // 2, k % 2
    y, zl = t % 4, t // 4
    hid = h_ref.shape[1]
    feat = g_ref.shape[1]
    rank = a_ref.shape[0]
    tiles = hid // TILE
    chips = 8
    out_q, in_q = (out0, out1, out2), (in0, in1, in2)

    widths = [ref.shape[2] - 128 for ref in in_q]
    starts = [0, widths[0], widths[0] + widths[1]]

    def across(j):
        return {"fsdp": 2 * j + c, "tp": t}

    def along(tt):
        return {"fsdp": fs, "tp": tt}

    sibling = {"fsdp": 2 * k + 1 - c, "tp": t}

    def slot(b):
        return store[ids[b]]

    def place(s):
        return (s % 2) * chips + s // 2

    def send(src, dst, s_sem, r_sem, dev):
        return pltpu.make_async_remote_copy(
            src_ref=src, dst_ref=dst, send_sem=s_sem, recv_sem=r_sem,
            device_id=dev, device_id_type=MESH,
        )

    def others(me, body):
        def step(i, _):
            body(lax.rem(me + i, chips))
            return 0

        lax.fori_loop(1, chips, step, 0)

    def loop(n, body):
        def step(i, _):
            body(i)
            return 0

        lax.fori_loop(0, n, step, 0)

    def corner(j):
        xj = j // 2
        return ((xj + 1) // 2) % 2, xj // 2, j % 2

    here = corner(k)
    beside = (2 * (x + 1 - 2 * (x % 2)) + zh, 2 * (3 - x) + zh, 2 * x + 1 - zh)
    orders = ((0, 1, 2), (1, 2, 0), (2, 0, 1))

    def apart(j, p):
        there = corner(j)
        return [(here[d] + there[d]) % 2 for d in orders[p]]

    barrier = pltpu.get_barrier_semaphore()
    pl.semaphore_signal(barrier, inc=1, device_id=sibling, device_id_type=MESH)
    others(k, lambda j: pl.semaphore_signal(barrier, inc=1, device_id=across(j), device_id_type=MESH))
    others(t, lambda j: pl.semaphore_signal(barrier, inc=1, device_id=along(j), device_id_type=MESH))

    mine = pl.ds(pl.multiple_of(c * feat, feat), feat)

    def w_rows(p):
        return pl.ds(starts[p], widths[p])

    def w_here(p):
        return pltpu.make_async_copy(w_ref.at[w_rows(p)], w_all.at[w_rows(p), mine], wl.at[p])

    def w_out(p):
        return send(w_ref.at[w_rows(p)], w_all.at[w_rows(p), mine], ws.at[p], wr.at[p], sibling)

    for p in range(3):
        w_here(p).start()

    def masked(j):
        rows = lax.broadcasted_iota(jnp.int32, (BLOCK, feat), 0)
        g = g_ref[pl.ds(pl.multiple_of(j * BLOCK, BLOCK), BLOCK), :]
        return jnp.where(rows < live[2 * t + j], g, jnp.zeros((), bf16))

    dy[y, zl, :, mine] = masked(c)
    stage[...] = masked(1 - c)
    pl.semaphore_wait(barrier, 15)

    to_sib = send(stage, dy.at[y, zl, :, mine], ss.at[0], sr.at[0], sibling)
    to_sib.start()
    for p in range(3):
        w_out(p).start()
    to_sib.wait_recv()

    y_next, y_prev, y_far = lax.rem(y + 1, 4), lax.rem(y + 3, 4), lax.rem(y + 2, 4)

    def dy_send(yy, zz, n, tt):
        return send(dy.at[yy, zz], dy.at[yy, zz], gs.at[0, n], gr.at[0, zz * 4 + yy], along(tt))

    def dy_half(yy, zz, half, tt):
        rows = pl.ds(half * (BLOCK // 2), BLOCK // 2)
        piece = dy.at[yy, zz, rows]
        return send(piece, piece, gs.at[1, half * 2 + zz], gr.at[1 + half, zz * 4 + yy], along(tt))

    def dy_wait(yy, zz):
        send(dy.at[yy, zz], dy.at[yy, zz], gs.at[0, 0], gr.at[0, zz * 4 + yy], sibling).wait_recv()

    own = [dy_send(y, zl, 0, (1 - zl) * 4 + y)]
    own += [dy_send(y, zl, 1 + i, zl * 4 + yy) for i, yy in enumerate((y_next, y_prev))]
    for cp in own:
        cp.start()

    def a_copy(j):
        return send(a_ref, a_all.at[c * chips + k], gs.at[2, j], gr.at[3, k], across(j))

    def b_copy(j):
        cols = pl.ds(pl.multiple_of(j * 2 * feat, 2 * feat), 2 * feat)
        return send(b_ref.at[:, cols], b_all.at[c * chips + k], gs.at[3, j], gr.at[4, k], across(j))

    a_all[c * chips + k] = a_ref[...]
    b_all[c * chips + k] = b_ref[:, pl.ds(pl.multiple_of(k * 2 * feat, 2 * feat), 2 * feat)]

    dy_wait(y, 1 - zl)
    relay = [dy_send(y, 1 - zl, 3 + i, zl * 4 + yy) for i, yy in enumerate((y_next, y_prev))]
    for cp in relay:
        cp.start()
    others(k, lambda j: a_copy(j).start())
    others(k, lambda j: b_copy(j).start())

    half = pl.ds(c * chips, chips)
    a_fwd = send(a_all.at[half], a_all.at[half], ss.at[1], sr.at[1], sibling)
    b_fwd = send(b_all.at[half], b_all.at[half], ss.at[2], sr.at[2], sibling)

    def y_of(s):
        return lax.rem(y + s + (s // 2) * (5 - 2 * s), 4)

    def q_send(p, j, at, d):
        return send(out_q[p].at[j], in_q[p].at[at], qs.at[p, j], qr.at[p, at], across(beside[d]))

    def q_wait(p, at):
        send(out_q[p].at[0], in_q[p].at[at], qs.at[p, 0], qr.at[p, at], sibling).wait_recv()

    def cols(p, n):
        return pl.ds(pl.multiple_of(starts[p] + n * TILE, TILE), TILE)

    def inner(n):
        return pl.ds(pl.multiple_of(n * TILE, TILE), TILE)

    def code_and_send(s, zz, p, j, at, d):
        rows = pl.ds(zz * BLOCK, BLOCK)

        def top(n, peak):
            v = jnp.abs(part[s, rows, cols(p, n)])
            return jnp.maximum(peak, jnp.maximum(v[:, :128], v[:, 128:]))

        peak = lax.fori_loop(0, widths[p] // TILE, top, jnp.zeros((BLOCK, 128), f32))
        level = level_of(jnp.max(peak, axis=1, keepdims=True))
        gain = TOP * jnp.exp(level * (-1.0 / STEPS))

        def code(n):
            q = jnp.round(part[s, rows, cols(p, n)] * gain)
            out_q[p][j, :, inner(n)] = q.astype(jnp.int32).astype(jnp.int16)

        loop(widths[p] // TILE, code)
        marks = jnp.broadcast_to(level, (BLOCK, 128))
        out_q[p][j, :, widths[p] :] = marks.astype(jnp.int32).astype(jnp.int16)
        q_send(p, j, at, d).start()

    def fold(s, zz, p, at, dst):
        q_wait(p, at)
        scale = jnp.exp(in_q[p][at, :, widths[p] :].astype(f32) * (1.0 / STEPS)) * (1.0 / TOP)
        scale = jnp.concatenate([scale, scale], axis=1)
        rows = pl.ds(zz * BLOCK, BLOCK)

        def add(n):
            v = part[s, rows, cols(p, n)] + in_q[p][at, :, inner(n)].astype(f32) * scale
            if dst is None:
                part[s, rows, cols(p, n)] = v
            else:
                dst[:, cols(p, n)] = v

        loop(widths[p] // TILE, add)

    def stage1(s):
        yy = y_of(s)
        for p in range(3):
            @pl.when(s == 0)
            def _():
                w_here(p).wait()
                w_out(p).wait_recv()

            def tile(n):
                at = cols(p, n)
                part[s, :, at] = nt(dy[yy].reshape(2 * BLOCK, 2 * feat), w_all[at, :])

            loop(widths[p] // TILE, tile)
            for zz in range(2):
                j = zz * 4 + yy
                r1, r2, r3 = apart(j, p)

                @pl.when(r1 == 1)
                def _():
                    code_and_send(s, zz, p, j, r2 * 2 + r3, orders[p][0])

    def stage2(s):
        yy = y_of(s)
        for p in range(3):
            for zz in range(2):
                j = zz * 4 + yy
                r1, r2, r3 = apart(j, p)

                @pl.when(r1 == 0)
                def _():
                    fold(s, zz, p, r2 * 2 + r3, None)

                    @pl.when(r2 == 1)
                    def _():
                        code_and_send(s, zz, p, j, 4 + r3, orders[p][1])

    def stage3(s):
        yy = y_of(s)
        for p in range(3):
            for zz in range(2):
                j = zz * 4 + yy
                r1, r2, r3 = apart(j, p)

                @pl.when(r1 + r2 == 0)
                def _():
                    fold(s, zz, p, 4 + r3, None)

                    @pl.when(r3 == 1)
                    def _():
                        code_and_send(s, zz, p, j, 6, orders[p][2])

    def stage4(s):
        yy = y_of(s)
        for p in range(3):
            for zz in range(2):
                @pl.when(zz * 4 + yy == k)
                def _():
                    fold(s, zz, p, 6, acc)

    def lin_copy(j):
        return send(lin_part.at[t], lin_part.at[t], gs.at[4, j], gr.at[5, t], along(j))

    def lin_all_copy(j):
        return send(lin_own, lin_all.at[k], gs.at[5, j], gr.at[6, k], across(j))

    def low_copy(j):
        return send(low_part.at[j], low_in_parts.at[k], gs.at[6, j], gr.at[7, k], across(j))

    def da_copy(j):
        return send(da_own, da_all.at[k], gs.at[7, j], gr.at[8, k], across(j))

    def ob_copy(j):
        return send(slot_terms.at[c, j], slot_all.at[t, k], gs.at[8, j], gr.at[9, k], across(j))

    def ob_along(tt, n, to):
        return send(slot_all.at[tt], slot_all.at[tt], gs.at[9, n], gr.at[10, tt], along(to))

    def ob_wait(tt):
        send(slot_all.at[tt], slot_all.at[tt], gs.at[9, 0], gr.at[10, tt], sibling).wait_recv()

    slot_swap = send(slot_terms.at[1 - c], slot_other, ss.at[3], sr.at[3], sibling)
    da_swap = send(da_send, da_other, ss.at[4], sr.at[4], sibling)
    ob_own = [ob_along(t, 0, (1 - zl) * 4 + y)]
    ob_own += [ob_along(t, 1 + i, zl * 4 + yy) for i, yy in enumerate((y_next, y_prev, y_far))]
    t_z = (1 - zl) * 4 + y
    ob_relay = [ob_along(t_z, 4 + i, zl * 4 + yy) for i, yy in enumerate((y_next, y_prev, y_far))]
    halves = [dy_half(y_next, zz, 0, zl * 4 + y_prev) for zz in range(2)]
    halves += [dy_half(y_prev, zz, 1, zl * 4 + y_next) for zz in range(2)]

    def take_neighbours():
        for zz in (zl, 1 - zl):
            dy_wait(y_next, zz)
            dy_half(y_next, zz, 0, zl * 4 + y_prev).start()
            dy_wait(y_prev, zz)
            dy_half(y_prev, zz, 1, zl * 4 + y_next).start()

    def take_far():
        for zz in (zl, 1 - zl):
            for side in range(2):
                dy_half(y_far, zz, side, zl * 4 + y_next).wait_recv()

    def share_adapters():
        others(k, lambda j: send(a_ref, a_all.at[c * chips + j], gs.at[2, j], gr.at[3, j], across(j)).wait_recv())
        a_fwd.start()
        others(k, lambda j: send(b_ref.at[:, : 2 * feat], b_all.at[c * chips + j], gs.at[3, j], gr.at[4, j], across(j)).wait_recv())
        b_fwd.start()

    def low_activations():
        a_fwd.wait_recv()
        a_sel[...] = a_all[place(slot(fs))]
        lin_part[t] = nt(a_sel[...], h_ref[...])
        others(t, lambda j: lin_copy(j).start())

    def share_low_activations():
        others(t, lambda j: send(lin_part.at[j], lin_part.at[j], gs.at[4, j], gr.at[5, j], along(j)).wait_recv())
        total = lin_part[0]
        for j in range(1, chips):
            total = total + lin_part[j]
        lin_own[...] = (adapter_scale * total).astype(bf16)
        others(k, lambda j: lin_all_copy(j).start())
        lin_all[k] = lin_own[...]

    def low_cotangents():
        b_fwd.wait_recv()

        def low_step(j):
            low_part[j] = nt(b_all[place(slot(2 * j + c))], dy[j % 4, j // 4])

        loop(chips, low_step)
        others(k, lambda j: low_copy(j).start())
        low_in_parts[k] = low_part[k]

    def output_map_terms():
        others(k, lambda j: send(lin_own, lin_all.at[j], gs.at[5, j], gr.at[6, j], across(j)).wait_recv())
        for j in range(chips):
            at = ((j % 4) * 2 + j // 4) * BLOCK
            s = slot(2 * j + c)
            value = lin_all[j]
            for n in range(2 * chips):
                hit = (s == 2 * (n % chips) + n // chips).astype(f32).astype(bf16)
                spread[n * rank : (n + 1) * rank, at : at + BLOCK] = value * hit
        share = slot_terms.shape[3]
        cut = pl.ds(pl.multiple_of(t * share, share), share)
        terms = nn(spread[...], dy[:, :, :, cut].reshape(chips * BLOCK, share))
        slot_terms[...] = terms.reshape(2, chips, rank, share)
        slot_swap.start()

    def output_map_sums():
        slot_swap.wait_recv()
        slot_terms[c] = slot_terms[c] + slot_other[...]
        others(k, lambda j: ob_copy(j).start())
        slot_all[t, k] = slot_terms[c, k]

    def output_map_share():
        others(k, lambda j: send(slot_terms.at[c, j], slot_all.at[t, j], gs.at[8, j], gr.at[9, j], across(j)).wait_recv())
        for cp in ob_own:
            cp.start()

    def output_map_relay():
        ob_wait(t_z)
        for cp in ob_relay:
            cp.start()

    def input_map_terms():
        others(k, lambda j: send(low_part.at[j], low_in_parts.at[j], gs.at[6, j], gr.at[7, j], across(j)).wait_recv())
        total = low_in_parts[0]
        for j in range(1, chips):
            total = total + low_in_parts[j]
        low = (adapter_scale * total).astype(bf16)
        low_kept[...] = low
        da = nn(low, h_ref[...])
        level = level_of(jnp.max(jnp.abs(da), axis=1, keepdims=True))
        gain = TOP * jnp.exp(level * (-1.0 / STEPS))
        da_own[:, :hid] = jnp.round(da * gain).astype(jnp.int32).astype(jnp.int16)
        da_own[:, hid:] = jnp.broadcast_to(level, (rank, 128)).astype(jnp.int32).astype(jnp.int16)
        others(k, lambda j: da_copy(j).start())
        da_all[k] = da_own[...]

    def da_sum(s):
        out = jnp.zeros((rank, hid), f32)
        for j in range(chips):
            hit = (slot(2 * j + c) == s).astype(f32) * (1.0 / TOP)
            scale = jnp.exp(da_all[j, :, hid:].astype(f32) * (1.0 / STEPS))[:, :1] * hit
            out = out + da_all[j, :, :hid].astype(f32) * scale
        return out

    def input_map_sums():
        others(k, lambda j: send(da_own, da_all.at[j], gs.at[7, j], gr.at[8, j], across(j)).wait_recv())
        da_send[...] = da_sum(2 * k + 1 - c)
        da_swap.start()
        o_a[...] = da_sum(2 * k + c)

    plan = (
        ((), ()),
        ((take_neighbours,), (share_adapters,)),
        ((), (low_activations,)),
        ((share_low_activations, take_far, low_cotangents), (output_map_terms,)),
        ((input_map_terms, output_map_sums), ()),
        ((output_map_share,), ()),
        ((output_map_relay, input_map_sums), ()),
    )

    def when(cond, body):
        pl.when(cond)(body)

    def step(it):
        for i, (before, _) in enumerate(plan):
            if before:
                when(it == i, lambda: [f() for f in before] and None)
        when(it < 4, lambda: stage1(it))
        for i, (_, after) in enumerate(plan):
            if after:
                when(it == i, lambda: [f() for f in after] and None)
        when((it >= 1) & (it < 5), lambda: stage2(it - 1))
        when((it >= 2) & (it < 6), lambda: stage3(it - 2))
        when(it >= 3, lambda: stage4(it - 3))

    loop(7, step)

    low_rows = low_kept[...].astype(f32).T.astype(bf16)

    def finish(n):
        at = inner(n)
        o_h[:, at] = (acc[:, at] + nn(low_rows, a_sel[:, at])).astype(bf16)

    loop(tiles, finish)

    da_swap.wait_recv()
    o_a[...] += da_other[...]

    others(t, lambda j: pl.when(j != t_z)(lambda: ob_wait(j)))
    share = slot_terms.shape[3]

    def put(i):
        tt, j = i % chips, i // chips
        o_b[:, pl.ds(pl.multiple_of(i * share, share), share)] = slot_all[tt, j]

    loop(chips * chips, put)

    for cp in (to_sib, a_fwd, b_fwd, slot_swap, da_swap, *own, *relay, *halves, *ob_own, *ob_relay):
        cp.wait_send()
    for p in range(3):
        w_out(p).wait_send()
        others(k, lambda j: q_send(p, j, 0, 0).wait_send())
    for copy in (a_copy, b_copy, lin_all_copy, low_copy, da_copy, ob_copy):
        others(k, lambda j: copy(j).wait_send())
    others(t, lambda j: lin_copy(j).wait_send())


def local(h, g, w, a, b, ids, live, store):
    tok, hid = h.shape
    feat = g.shape[1]
    rank = a.shape[2]
    wide = b.shape[2]
    chips = 8
    share = 2 * feat // chips
    third = hid // (3 * TILE) * TILE
    widths = (hid - 2 * third, third, third)
    a_t = jnp.swapaxes(a, 1, 2).reshape(rank, hid)
    vm = pl.BlockSpec(memory_space=pltpu.VMEM)
    sm = pl.BlockSpec(memory_space=pltpu.SMEM)
    dma = pltpu.SemaphoreType.DMA
    o_h, o_a, o_b = pl.pallas_call(
        kernel,
        out_shape=(
            jax.ShapeDtypeStruct((tok, hid), bf16),
            jax.ShapeDtypeStruct((rank, hid), f32),
            jax.ShapeDtypeStruct((rank, wide), f32),
        ),
        in_specs=[sm, sm, sm, vm, vm, pl.BlockSpec(memory_space=pl.ANY), vm, vm],
        out_specs=(vm, vm, vm),
        scratch_shapes=[
            pltpu.VMEM((hid, 2 * feat), bf16),
            pltpu.VMEM((4, 2, BLOCK, 2 * feat), bf16),
            pltpu.VMEM((BLOCK, feat), bf16),
            pltpu.VMEM((4, 2 * BLOCK, hid), f32),
            pltpu.VMEM((BLOCK, hid), f32),
            *[pltpu.VMEM((chips, BLOCK, w + 128), jnp.int16) for w in widths],
            *[pltpu.VMEM((chips - 1, BLOCK, w + 128), jnp.int16) for w in widths],
            pltpu.VMEM((2 * chips, rank, hid), bf16),
            pltpu.VMEM((2 * chips, rank, 2 * feat), bf16),
            pltpu.VMEM((rank, hid), bf16),
            pltpu.VMEM((chips, rank, BLOCK), f32),
            pltpu.VMEM((rank, BLOCK), bf16),
            pltpu.VMEM((chips, rank, BLOCK), bf16),
            pltpu.VMEM((chips, rank, BLOCK), f32),
            pltpu.VMEM((chips, rank, BLOCK), f32),
            pltpu.VMEM((2, chips, rank, share), f32),
            pltpu.VMEM((chips, rank, share), f32),
            pltpu.VMEM((chips, chips, rank, share), f32),
            pltpu.VMEM((rank, hid + 128), jnp.int16),
            pltpu.VMEM((chips, rank, hid + 128), jnp.int16),
            pltpu.VMEM((rank, hid), f32),
            pltpu.VMEM((rank, hid), f32),
            pltpu.VMEM((rank, BLOCK), bf16),
            pltpu.VMEM((2 * chips * rank, chips * BLOCK), bf16),
            dma((10, 8)),
            dma((11, 8)),
            dma((3, 8)),
            dma((3, 7)),
            dma((3,)),
            dma((3,)),
            dma((3,)),
            dma((5,)),
            dma((5,)),
        ],
        compiler_params=pltpu.CompilerParams(
            collective_id=0, has_side_effects=True, vmem_limit_bytes=62 << 20
        ),
    )(ids, live, store, h, g, w, a_t, b.reshape(rank, wide))
    return (
        o_h,
        jnp.swapaxes(o_a.reshape(1, rank, hid), 1, 2),
        o_b.reshape(1, rank, wide),
    )


def solution(mesh):
    placed = (
        P("fsdp", "tp"),
        P("tp", "fsdp"),
        P("tp", "fsdp"),
        P("fsdp", "tp", None),
        P("fsdp", None, None),
        P(),
        P(),
        P(),
    )
    return jax.shard_map(
        local,
        mesh=mesh,
        in_specs=placed,
        out_specs=(P("fsdp", "tp"), P("fsdp", "tp", None), P("fsdp", None, None)),
        check_vma=False,
    )
```

```python
import functools
import math

import jax
import jax.numpy as jnp
from jax import lax
from jax.experimental import pallas as pl
from jax.experimental.pallas import tpu as pltpu
from jax.sharding import PartitionSpec as P

BLOCK = 128
TILE = 256
MESH = pl.DeviceIdType.MESH
adapter_scale = 2.0
f32 = jnp.float32
bf16 = jnp.bfloat16

TOP = 32000.0
STEPS = 8.0 / math.log(2.0)


def nt(a, b):
    return lax.dot_general(a, b, (((1,), (1,)), ((), ())), preferred_element_type=f32)


def nn(a, b):
    return lax.dot_general(a, b, (((1,), (0,)), ((), ())), preferred_element_type=f32)


def level_of(peak):
    return jnp.ceil(jnp.log(jnp.maximum(peak, 1e-30)) * STEPS)


def widths_of(hid):
    tiles = hid // TILE
    return [(tiles * (p + 1) // 6 - tiles * p // 6) * TILE for p in range(6)][::-1]


def keep(h, a, b, o_h, o_a, o_b, v_h, v_a, v_b, came, left):
    ways = ((h, v_h, o_h), (b, v_b, o_b), (a, v_a, o_a))
    into = [pltpu.make_async_copy(x, v, came.at[i]) for i, (x, v, _) in enumerate(ways)]
    out = [pltpu.make_async_copy(v, o, left.at[i]) for i, (_, v, o) in enumerate(ways)]
    for cp in into:
        cp.start()
    for first, second in zip(into, out):
        first.wait()
        second.start()
    for cp in out:
        cp.wait()


def kernel(
    ids, live, store, h_ref, g_ref, w_ref, a_ref, b_ref,
    o_h, o_a, o_b,
    w_all, dy, stage, part, out_q, in_q, out_m, in_m, h_in, g_in, a_all, b_all, a_sel,
    lin_part, lin_own, lin_block, own_terms, all_terms, low_part, low_in_parts, low_rows, eye, slot_terms, slot_other, slot_all,
    da_blocks, da_out, da_in, da_sum, a_over_out, a_over_in, b_over_out, b_over_in, low_kept,
    gs, gr, qs, qr, ms, mr, ws, wr, wl, ls, ss, sr,
):
    fs = lax.axis_index("fsdp")
    t = lax.axis_index("tp")
    k, c = fs // 2, fs % 2
    x, zh = k // 2, k % 2
    y, zl = t % 4, t // 4
    hid = h_ref.shape[1]
    feat = g_ref.shape[1]
    rank = a_ref.shape[0]
    chips = 8
    share = 2 * feat // chips

    widths = widths_of(hid)
    starts = [sum(widths[:p]) for p in range(len(widths))]

    def across(j):
        return {"fsdp": 2 * j + c, "tp": t}

    def along(tt):
        return {"fsdp": fs, "tp": tt}

    sibling = {"fsdp": 2 * k + 1 - c, "tp": t}

    def slot(b):
        return store[ids[b]]

    def send(src, dst, s_sem, r_sem, dev):
        return pltpu.make_async_remote_copy(
            src_ref=src, dst_ref=dst, send_sem=s_sem, recv_sem=r_sem,
            device_id=dev, device_id_type=MESH,
        )

    def others(me, body):
        def step(i, _):
            body(lax.rem(me + i, chips))
            return 0

        lax.fori_loop(1, chips, step, 0)

    def loop(n, body):
        def step(i, _):
            body(i)
            return 0

        lax.fori_loop(0, n, step, 0)

    def corner(j):
        xj = j // 2
        return ((xj + 1) // 2) % 2, xj // 2, j % 2

    here = corner(k)
    beside = (2 * (x + 1 - 2 * (x % 2)) + zh, 2 * (3 - x) + zh, 2 * x + 1 - zh)
    orders = ((0, 1, 2), (1, 2, 0), (2, 0, 1), (0, 2, 1), (1, 0, 2), (1, 2, 0))

    def apart(j, p):
        there = corner(j)
        return [(here[d] + there[d]) % 2 for d in orders[p]]

    mine = pl.ds(pl.multiple_of(c * feat, feat), feat)

    def b_cols(xx):
        return pl.ds(pl.multiple_of(xx * 4 * feat, 4 * feat), 4 * feat)

    load_g = pltpu.make_async_copy(g_ref, g_in, ls.at[0])
    load_h = pltpu.make_async_copy(h_ref, h_in, ls.at[1])
    load_a = pltpu.make_async_copy(a_ref, a_all.at[c, x], ls.at[2])
    load_b = pltpu.make_async_copy(b_ref.at[:, b_cols(x)], b_all.at[c, x], ls.at[3])

    load_g.start()
    corners = [lax.broadcasted_iota(jnp.int32, (BLOCK, BLOCK), d) for d in range(2)]
    eye[...] = (corners[0] == corners[1]).astype(f32)

    barrier = pltpu.get_barrier_semaphore()
    pl.semaphore_signal(barrier, inc=1, device_id=sibling, device_id_type=MESH)
    others(k, lambda j: pl.semaphore_signal(barrier, inc=1, device_id=across(j), device_id_type=MESH))
    others(t, lambda j: pl.semaphore_signal(barrier, inc=1, device_id=along(j), device_id_type=MESH))

    def w_rows(p):
        return pl.ds(starts[p], widths[p])

    def w_here(p):
        return pltpu.make_async_copy(w_ref.at[w_rows(p)], w_all.at[w_rows(p), mine], wl.at[p])

    def w_out(p):
        return send(w_ref.at[w_rows(p)], w_all.at[w_rows(p), mine], ws.at[p], wr.at[p], sibling)

    for p in range(len(widths)):
        w_here(p).start()

    for cp in (load_b, load_a, load_h):
        cp.start()
    load_g.wait()

    def masked(j):
        rows = lax.broadcasted_iota(jnp.int32, (BLOCK, feat), 0)
        g = g_in[pl.ds(pl.multiple_of(j * BLOCK, BLOCK), BLOCK), :]
        return jnp.where(rows < live[2 * t + j], g, jnp.zeros((), bf16))

    dy[y, zl, :, mine] = masked(c)
    stage[...] = masked(1 - c)
    pl.semaphore_wait(barrier, 15)

    to_sib = send(stage, dy.at[y, zl, :, mine], ss.at[0], sr.at[0], sibling)
    to_sib.start()
    for p in range(len(widths)):
        w_out(p).start()
    to_sib.wait_recv()

    y_next, y_prev, y_far = lax.rem(y + 1, 4), lax.rem(y + 3, 4), lax.rem(y + 2, 4)

    def dy_send(yy, zz, n, tt):
        return send(dy.at[yy, zz], dy.at[yy, zz], gs.at[0, n], gr.at[0, zz * 4 + yy], along(tt))

    def dy_half(yy, zz, half, tt):
        rows = pl.ds(half * (BLOCK // 2), BLOCK // 2)
        piece = dy.at[yy, zz, rows]
        return send(piece, piece, gs.at[1, half * 2 + zz], gr.at[1 + half, zz * 4 + yy], along(tt))

    def dy_wait(yy, zz):
        send(dy.at[yy, zz], dy.at[yy, zz], gs.at[0, 0], gr.at[0, zz * 4 + yy], sibling).wait_recv()

    own = [dy_send(y, zl, 0, (1 - zl) * 4 + y)]
    own += [dy_send(y, zl, 1 + i, zl * 4 + yy) for i, yy in enumerate((y_next, y_prev))]
    for cp in own:
        cp.start()

    def a_copy(xx):
        return send(a_ref, a_all.at[c, x], gs.at[2, xx], gr.at[3, x], across(2 * xx + zh))

    def b_copy(xx):
        return send(b_ref.at[:, b_cols(xx)], b_all.at[c, x], gs.at[3, xx], gr.at[4, x], across(2 * xx + zh))

    def others_x(body):
        for n in range(1, 4):
            body(lax.rem(x + n, 4))

    others_x(lambda xx: a_copy(xx).start())
    others_x(lambda xx: b_copy(xx).start())

    relay = [dy_send(y, 1 - zl, 3 + i, zl * 4 + yy) for i, yy in enumerate((y_next, y_prev))]

    def take_z():
        dy_wait(y, 1 - zl)
        for cp in relay:
            cp.start()
        take_near(zl)

    partner = across(2 * x + 1 - zh)
    a_fwd = send(a_all.at[c], a_all.at[c], ss.at[1], sr.at[1], sibling)
    b_fwd = send(b_all.at[c], b_all.at[c], ss.at[2], sr.at[2], sibling)
    a_over = send(a_over_out, a_over_in, ss.at[7], sr.at[7], partner)
    b_over = send(b_over_out, b_over_in, ss.at[8], sr.at[8], partner)

    def y_of(s):
        return lax.rem(y + s + (s // 2) * (5 - 2 * s), 4)

    def q_send(p, j, at, d):
        w = widths[p]
        return send(out_q.at[p, j, :, :w], in_q.at[p, at, :, :w], qs.at[p, j], qr.at[p, at], across(beside[d]))

    def m_send(p, j, at, d):
        return send(out_m.at[p, j], in_m.at[p, at], ms.at[p, j], mr.at[p, at], across(beside[d]))

    def cols(p, n):
        return pl.ds(pl.multiple_of(starts[p] + n * TILE, TILE), TILE)

    def inner(n):
        return pl.ds(pl.multiple_of(n * TILE, TILE), TILE)

    def code_and_send(s, zz, p, j, at, d):
        rows = pl.ds(pl.multiple_of(zz * BLOCK, BLOCK), BLOCK)

        def top(n, peak):
            v = jnp.abs(part[s, rows, cols(p, n)])
            return jnp.maximum(peak, jnp.maximum(v[:, :128], v[:, 128:]))

        peak = lax.fori_loop(0, widths[p] // TILE, top, jnp.zeros((BLOCK, 128), f32))
        level = level_of(jnp.max(peak, axis=1, keepdims=True))
        gain = TOP * jnp.exp(level * (-1.0 / STEPS))

        def code(n):
            q = jnp.round(part[s, rows, cols(p, n)] * gain)
            out_q[p, j, :, inner(n)] = q.astype(jnp.int32).astype(jnp.int16)

        out_m[p, j] = jnp.broadcast_to(jnp.sum(eye[...] * level, axis=0, keepdims=True), (8, BLOCK))
        m_send(p, j, at, d).start()
        loop(widths[p] // TILE, code)
        q_send(p, j, at, d).start()

    def fold(s, zz, p, at, last):
        m_send(p, 0, at, 0).wait_recv()
        level = jnp.sum(eye[...] * in_m[p, at][:1], axis=1, keepdims=True)
        scale = jnp.exp(level * (1.0 / STEPS)) * (1.0 / TOP)
        scale = jnp.broadcast_to(scale, (BLOCK, TILE))
        rows = pl.ds(pl.multiple_of(zz * BLOCK, BLOCK), BLOCK)
        q_send(p, 0, at, 0).wait_recv()

        def add(n):
            v = part[s, rows, cols(p, n)] + in_q[p, at, :, inner(n)].astype(f32) * scale
            if last:
                v = v + nn(low_rows[...], a_sel[:, cols(p, n)])
                o_h[:, cols(p, n)] = v.astype(bf16)
            else:
                part[s, rows, cols(p, n)] = v

        loop(widths[p] // TILE, add)

    def stage1(s):
        yy = y_of(s)
        for p in range(len(widths)):
            at = w_rows(p)
            part[s, :, at] = nt(dy[yy].reshape(2 * BLOCK, 2 * feat), w_all[at, :])
            for zz in range(2):
                j = zz * 4 + yy
                r1, r2, r3 = apart(j, p)

                @pl.when(r1 == 1)
                def _():
                    code_and_send(s, zz, p, j, r2 * 2 + r3, orders[p][0])

    def stage1_alone(i):
        zz = lax.rem(zl + i, 2)
        j = zz * 4 + y
        rows = pl.ds(pl.multiple_of(zz * BLOCK, BLOCK), BLOCK)

        @pl.when(i == 1)
        def _():
            take_z()

        for p in range(len(widths)):
            @pl.when(i == 0)
            def _():
                w_here(p).wait()
                w_out(p).wait_recv()

            at = w_rows(p)
            part[0, rows, at] = nt(dy[y, zz], w_all[at, :])
            r1, r2, r3 = apart(j, p)

            @pl.when(r1 == 1)
            def _():
                code_and_send(0, zz, p, j, r2 * 2 + r3, orders[p][0])

    def stage2(s):
        yy = y_of(s)
        for p in range(len(widths)):
            for zz in range(2):
                j = zz * 4 + yy
                r1, r2, r3 = apart(j, p)

                @pl.when(r1 == 0)
                def _():
                    fold(s, zz, p, r2 * 2 + r3, False)

                    @pl.when(r2 == 1)
                    def _():
                        code_and_send(s, zz, p, j, 4 + r3, orders[p][1])

    def stage3(s):
        yy = y_of(s)
        for p in range(len(widths)):
            for zz in range(2):
                j = zz * 4 + yy
                r1, r2, r3 = apart(j, p)

                @pl.when(r1 + r2 == 0)
                def _():
                    fold(s, zz, p, 4 + r3, False)

                    @pl.when(r3 == 1)
                    def _():
                        code_and_send(s, zz, p, j, 6, orders[p][2])

    def stage4(s):
        yy = y_of(s)
        for p in range(len(widths)):
            for zz in range(2):
                @pl.when(zz * 4 + yy == k)
                def _():
                    fold(s, zz, p, 6, True)

    def lin_copy(j):
        return send(lin_part.at[t], lin_part.at[t], gs.at[4, j], gr.at[5, t], along(j))

    def lin_block_copy(j):
        return send(lin_own, lin_block, gs.at[5, j], sr.at[6], across(j))

    low_out_copy = send(low_part, low_in_parts.at[k], ss.at[5], gr.at[7, k], across(t))

    def low_copy(tt):
        return send(low_kept, low_kept, gs.at[6, tt], sr.at[5], along(tt))

    def da_copy(xx):
        return send(da_out.at[xx], da_in.at[x], gs.at[7, xx], gr.at[8, x], across(2 * xx + zh))

    da_sib = send(da_blocks.at[0], da_blocks.at[1], ss.at[4], sr.at[4], sibling)
    da_over = send(da_blocks.at[0], da_blocks.at[2], ss.at[9], sr.at[9], partner)
    da_sib_over = send(da_blocks.at[2], da_blocks.at[3], ss.at[10], sr.at[10], sibling)

    def ob_copy(j):
        return send(slot_terms.at[c, j], slot_all.at[t, k], gs.at[8, j], gr.at[9, k], across(j))

    def ob_along(tt, n, to):
        return send(slot_all.at[tt], slot_all.at[tt], gs.at[9, n], gr.at[10, tt], along(to))

    def ob_wait(tt):
        send(slot_all.at[tt], slot_all.at[tt], gs.at[9, 0], gr.at[10, tt], sibling).wait_recv()

    slot_swap = send(slot_terms.at[1 - c], slot_other, ss.at[3], sr.at[3], sibling)
    ob_own = [ob_along(t, 0, (1 - zl) * 4 + y)]
    ob_own += [ob_along(t, 1 + i, zl * 4 + yy) for i, yy in enumerate((y_next, y_prev, y_far))]
    t_z = (1 - zl) * 4 + y
    ob_relay = [ob_along(t_z, 4 + i, zl * 4 + yy) for i, yy in enumerate((y_next, y_prev, y_far))]
    halves = [dy_half(y_next, zz, 0, zl * 4 + y_prev) for zz in range(2)]
    halves += [dy_half(y_prev, zz, 1, zl * 4 + y_next) for zz in range(2)]

    def take_near(zz):
        dy_wait(y_next, zz)
        dy_half(y_next, zz, 0, zl * 4 + y_prev).start()
        dy_wait(y_prev, zz)
        dy_half(y_prev, zz, 1, zl * 4 + y_next).start()

    def take_near_second():
        take_near(1 - zl)

    def take_far():
        for zz in (zl, 1 - zl):
            for side in range(2):
                dy_half(y_far, zz, side, zl * 4 + y_next).wait_recv()

    def share_adapters():
        others_x(lambda xx: send(a_ref, a_all.at[c, xx], gs.at[2, xx], gr.at[3, xx], sibling).wait_recv())
        load_a.wait()
        a_fwd.start()
        others_x(lambda xx: send(b_ref.at[:, b_cols(0)], b_all.at[c, xx], gs.at[3, xx], gr.at[4, xx], sibling).wait_recv())
        load_b.wait()
        b_fwd.start()

    def features(z):
        return pl.ds(pl.multiple_of(z * 2 * feat, 2 * feat), 2 * feat)

    def hand_over():
        a_fwd.wait_recv()
        s = slot(2 * (2 * x + 1 - zh) + c)
        a_over_out[...] = a_all[s % 2, s // 4]
        a_over.start()
        b_fwd.wait_recv()
        s = slot(2 * t + c)
        b_over_out[...] = b_all[s % 2, s // 4, :, features(1 - zh)]
        b_over.start()

    def low_activations():
        s = slot(fs)
        a_over.wait_recv()
        here_too = ((s // 2) % 2 == zh).astype(f32).astype(bf16)
        there = ((s // 2) % 2 != zh).astype(f32).astype(bf16)
        a_sel[...] = a_all[s % 2, s // 4] * here_too + a_over_in[...] * there
        load_h.wait()
        lin_part[t] = nt(a_sel[...], h_in[...])
        others(t, lambda j: lin_copy(j).start())

    def share_low_activations():
        others(t, lambda j: send(lin_part.at[j], lin_part.at[j], gs.at[4, j], gr.at[5, j], along(j)).wait_recv())
        total = lin_part[0]
        for j in range(1, chips):
            total = total + lin_part[j]
        lin_own[...] = (adapter_scale * total).astype(bf16)

        @pl.when(k == t)
        def _():
            others(k, lambda j: lin_block_copy(j).start())

    def low_cotangents():
        s = slot(2 * t + c)
        b_over.wait_recv()
        here_too = ((s // 2) % 2 == zh).astype(f32).astype(bf16)
        there = ((s // 2) % 2 != zh).astype(f32).astype(bf16)
        b_sel = b_all[s % 2, s // 4, :, features(zh)] * here_too + b_over_in[...] * there
        low_part[...] = nt(b_sel, dy[y, zl])

        @pl.when(k != t)
        def _():
            low_out_copy.start()

    def low_sum():
        @pl.when(k == t)
        def _():
            low_in_parts[k] = low_part[...]
            others(k, lambda j: send(low_part, low_in_parts.at[j], ss.at[5], gr.at[7, j], across(j)).wait_recv())
            total = low_in_parts[0]
            for j in range(1, chips):
                total = total + low_in_parts[j]
            low_kept[...] = (adapter_scale * total).astype(bf16)
            others(t, lambda j: low_copy(j).start())

    def output_map_terms():
        @pl.when(k != t)
        def _():
            send(lin_own, lin_block, ss.at[6], sr.at[6], across(t)).wait_recv()

        @pl.when(k == t)
        def _():
            lin_block[...] = lin_own[...]

        for n in range(chips):
            own_terms[n] = nn(lin_block[...], dy[y, zl, :, n * share : (n + 1) * share])
        others(t, lambda j: terms_copy(j).start())
        all_terms[t] = own_terms[t]

    def terms_copy(j):
        return send(own_terms.at[j], all_terms.at[t], gs.at[10, j], gr.at[6, t], along(j))

    def output_map_slots():
        others(t, lambda j: send(own_terms.at[j], all_terms.at[j], gs.at[10, j], gr.at[6, j], along(j)).wait_recv())
        slots = [slot(2 * j + c) for j in range(chips)]

        def one(n):
            s = 2 * lax.rem(n, chips) + n // chips
            out = jnp.zeros((rank, share), f32)
            for j in range(chips):
                out = out + all_terms[j] * (slots[j] == s).astype(f32)
            slot_terms[n // chips, lax.rem(n, chips)] = out

        loop(2 * chips, one)
        slot_swap.start()

    def output_map_sums():
        slot_swap.wait_recv()
        slot_terms[c] = slot_terms[c] + slot_other[...]
        others(k, lambda j: ob_copy(j).start())
        slot_all[t, k] = slot_terms[c, k]

    def output_map_share():
        others(k, lambda j: send(slot_terms.at[c, j], slot_all.at[t, j], gs.at[8, j], gr.at[9, j], across(j)).wait_recv())
        for cp in ob_own:
            cp.start()

    def output_map_relay():
        ob_wait(t_z)
        for cp in ob_relay:
            cp.start()

    def input_map_terms():
        @pl.when(k != t)
        def _():
            low_copy(k).wait_recv()

        low = low_kept[...]
        low_rows[...] = low.astype(f32).T.astype(bf16)
        da_code(nn(low, h_in[...]), da_blocks.at[0])
        da_sib.start()
        da_over.start()

    def da_code(v, ref):
        level = level_of(jnp.max(jnp.abs(v), axis=1, keepdims=True))
        gain = TOP * jnp.exp(level * (-1.0 / STEPS))
        ref[:, :hid] = jnp.round(v * gain).astype(jnp.int32).astype(jnp.int16)
        ref[:, hid:] = jnp.broadcast_to(level, (rank, 128)).astype(jnp.int32).astype(jnp.int16)

    def da_value(ref, gain):
        scale = jnp.exp(ref[:, hid:].astype(f32) * (1.0 / STEPS))[:, :1] * (gain * (1.0 / TOP))
        return ref[:, :hid].astype(f32) * scale

    def input_map_pass():
        da_over.wait_recv()
        da_sib_over.start()

    def input_map_sums():
        da_sib.wait_recv()
        da_sib_over.wait_recv()
        k_z = 2 * x + 1 - zh
        slots = [slot(b) for b in (fs, 2 * k + 1 - c, 2 * k_z + c, 2 * k_z + 1 - c)]

        def one(n):
            xx = lax.rem(x + n, 4)
            out = jnp.zeros((rank, hid), f32)
            for i in range(4):
                out = out + da_value(da_blocks.at[i], (slots[i] == 2 * (2 * xx + zh) + c).astype(f32))

            @pl.when(n == 0)
            def _():
                da_sum[...] = out

            @pl.when(n > 0)
            def _():
                da_code(out, da_out.at[xx])
                da_copy(xx).start()

        loop(4, one)

    def input_map_end():
        def one(n):
            xx = lax.rem(x + n, 4)
            send(da_out.at[xx], da_in.at[xx], gs.at[7, xx], gr.at[8, xx], sibling).wait_recv()
            da_sum[...] += da_value(da_in.at[xx], 1.0)
            return 0

        lax.fori_loop(1, 4, lambda n, _: one(n), 0)
        o_a[...] = da_sum[...]

    plan = {
        1: ((share_adapters, hand_over, take_near_second, low_activations, low_cotangents), (share_low_activations, low_sum), (), ()),
        2: ((), (output_map_terms, input_map_terms), (), (output_map_slots, input_map_pass)),
        3: ((take_far,), (output_map_sums, input_map_sums), (), (output_map_share,)),
        4: ((), (), (output_map_relay,), ()),
    }

    def when(cond, body):
        pl.when(cond)(body)

    def run(it, place):
        for i, spots in plan.items():
            if spots[place]:
                when(it == i, lambda: [f() for f in spots[place]] and None)

    def step(i):
        it = i + 1
        run(it, 0)
        when(it < 4, lambda: stage1(it))
        run(it, 1)
        when(it < 5, lambda: stage2(it - 1))
        run(it, 2)
        when((it >= 2) & (it < 6), lambda: stage3(it - 2))
        when(it >= 3, lambda: stage4(it - 3))
        run(it, 3)

    loop(2, stage1_alone)
    loop(6, step)

    input_map_end()
    others(t, lambda j: pl.when(j != t_z)(lambda: ob_wait(j)))

    def put(i):
        tt, j = i % chips, i // chips
        o_b[:, pl.ds(pl.multiple_of(i * share, share), share)] = slot_all[tt, j]

    loop(chips * chips, put)

    for cp in (to_sib, a_fwd, b_fwd, a_over, b_over, slot_swap, da_sib, da_over, da_sib_over, *own, *relay, *halves, *ob_own, *ob_relay):
        cp.wait_send()
    for p in range(len(widths)):
        w_out(p).wait_send()
        others(k, lambda j: m_send(p, j, 0, 0).wait_send())
        others(k, lambda j: q_send(p, j, 0, 0).wait_send())
    for copy in (a_copy, b_copy, da_copy):
        others_x(lambda xx: copy(xx).wait_send())
    others(k, lambda j: ob_copy(j).wait_send())
    others(t, lambda j: lin_copy(j).wait_send())
    others(t, lambda j: terms_copy(j).wait_send())

    @pl.when(k == t)
    def _():
        others(t, lambda j: low_copy(j).wait_send())
        others(k, lambda j: lin_block_copy(j).wait_send())

    @pl.when(k != t)
    def _():
        low_out_copy.wait_send()


def local(h, g, w, a, b, ids, live, store):
    tok, hid = h.shape
    feat = g.shape[1]
    rank = a.shape[2]
    wide = b.shape[2]
    chips = 8
    share = 2 * feat // chips
    widths = widths_of(hid)
    a_t = jnp.swapaxes(a, 1, 2).reshape(rank, hid)
    vm = pl.BlockSpec(memory_space=pltpu.VMEM)
    sm = pl.BlockSpec(memory_space=pltpu.SMEM)
    far = pl.BlockSpec(memory_space=pl.ANY)
    dma = pltpu.SemaphoreType.DMA
    o_h, o_a, o_b = pl.pallas_call(
        kernel,
        out_shape=(
            jax.ShapeDtypeStruct((tok, hid), bf16),
            jax.ShapeDtypeStruct((rank, hid), f32),
            jax.ShapeDtypeStruct((rank, wide), f32),
        ),
        in_specs=[sm, sm, sm] + [far] * 5,
        out_specs=(vm, vm, vm),
        scratch_shapes=[
            pltpu.VMEM((hid, 2 * feat), bf16),
            pltpu.VMEM((4, 2, BLOCK, 2 * feat), bf16),
            pltpu.VMEM((BLOCK, feat), bf16),
            pltpu.VMEM((4, 2 * BLOCK, hid), f32),
            pltpu.VMEM((6, chips, BLOCK, max(widths)), jnp.int16),
            pltpu.VMEM((6, chips - 1, BLOCK, max(widths)), jnp.int16),
            pltpu.VMEM((6, chips, 8, BLOCK), f32),
            pltpu.VMEM((6, chips - 1, 8, BLOCK), f32),
            pltpu.VMEM((BLOCK, hid), bf16),
            pltpu.VMEM((2 * BLOCK, feat), bf16),
            pltpu.VMEM((2, 4, rank, hid), bf16),
            pltpu.VMEM((2, 4, rank, 4 * feat), bf16),
            pltpu.VMEM((rank, hid), bf16),
            pltpu.VMEM((chips, rank, BLOCK), f32),
            pltpu.VMEM((rank, BLOCK), bf16),
            pltpu.VMEM((rank, BLOCK), bf16),
            pltpu.VMEM((chips, rank, share), f32),
            pltpu.VMEM((chips, rank, share), f32),
            pltpu.VMEM((rank, BLOCK), f32),
            pltpu.VMEM((chips, rank, BLOCK), f32),
            pltpu.VMEM((BLOCK, rank), bf16),
            pltpu.VMEM((BLOCK, BLOCK), f32),
            pltpu.VMEM((2, chips, rank, share), f32),
            pltpu.VMEM((chips, rank, share), f32),
            pltpu.VMEM((chips, chips, rank, share), f32),
            pltpu.VMEM((4, rank, hid + 128), jnp.int16),
            pltpu.VMEM((4, rank, hid + 128), jnp.int16),
            pltpu.VMEM((4, rank, hid + 128), jnp.int16),
            pltpu.VMEM((rank, hid), f32),
            pltpu.VMEM((rank, hid), bf16),
            pltpu.VMEM((rank, hid), bf16),
            pltpu.VMEM((rank, 2 * feat), bf16),
            pltpu.VMEM((rank, 2 * feat), bf16),
            pltpu.VMEM((rank, BLOCK), bf16),
            dma((11, 8)),
            dma((11, 8)),
            dma((6, 8)),
            dma((6, 7)),
            dma((6, 8)),
            dma((6, 7)),
            dma((6,)),
            dma((6,)),
            dma((6,)),
            dma((4,)),
            dma((11,)),
            dma((11,)),
        ],
        compiler_params=pltpu.CompilerParams(
            collective_id=0, has_side_effects=True, vmem_limit_bytes=62 << 20
        ),
    )(ids, live, store, h, g, w, a_t, b.reshape(rank, wide))
    o_h, o_a, o_b = pl.pallas_call(
        keep,
        out_shape=tuple(jax.ShapeDtypeStruct(o.shape, o.dtype) for o in (o_h, o_a, o_b)),
        in_specs=[far] * 3,
        out_specs=(far,) * 3,
        scratch_shapes=[pltpu.VMEM(o.shape, o.dtype) for o in (o_h, o_a, o_b)] + [dma((3,)), dma((3,))],
        compiler_params=pltpu.CompilerParams(vmem_limit_bytes=62 << 20),
    )(o_h, o_a, o_b)
    return (
        o_h,
        jnp.swapaxes(o_a.reshape(1, rank, hid), 1, 2),
        o_b.reshape(1, rank, wide),
    )


def solution(mesh):
    placed = (
        P("fsdp", "tp"),
        P("tp", "fsdp"),
        P("tp", "fsdp"),
        P("fsdp", "tp", None),
        P("fsdp", None, None),
        P(),
        P(),
        P(),
    )
    return jax.shard_map(
        local,
        mesh=mesh,
        in_specs=placed,
        out_specs=(P("fsdp", "tp"), P("fsdp", "tp", None), P("fsdp", None, None)),
        check_vma=False,
    )
```

```python
import functools
import math

import jax
import jax.numpy as jnp
from jax import lax
from jax.experimental import pallas as pl
from jax.experimental.pallas import tpu as pltpu
from jax.sharding import PartitionSpec as P

BLOCK = 128
TILE = 256
MESH = pl.DeviceIdType.MESH
adapter_scale = 2.0
f32 = jnp.float32
bf16 = jnp.bfloat16

TOP = 32000.0
STEPS = 8.0 / math.log(2.0)


def nt(a, b):
    return lax.dot_general(a, b, (((1,), (1,)), ((), ())), preferred_element_type=f32)


def nn(a, b):
    return lax.dot_general(a, b, (((1,), (0,)), ((), ())), preferred_element_type=f32)


def level_of(peak):
    return jnp.ceil(jnp.log(jnp.maximum(peak, 1e-30)) * STEPS)


def widths_of(hid):
    tiles = hid // TILE
    return [(tiles * (p + 1) // 6 - tiles * p // 6) * TILE for p in range(6)][::-1]


def keep(h, a, b, o_h, o_a, o_b, v_h, v_a, v_b, came, left):
    ways = ((h, v_h, o_h), (b, v_b, o_b), (a, v_a, o_a))
    into = [pltpu.make_async_copy(x, v, came.at[i]) for i, (x, v, _) in enumerate(ways)]
    out = [pltpu.make_async_copy(v, o, left.at[i]) for i, (_, v, o) in enumerate(ways)]
    for cp in into:
        cp.start()
    for first, second in zip(into, out):
        first.wait()
        second.start()
    for cp in out:
        cp.wait()


def kernel(
    ids, live, store, h_ref, g_ref, w_ref, a_ref, b_ref,
    o_h, o_a, o_b,
    w_all, dy, stage, part, out_q, in_q, h_in, g_in, a_all, b_all, a_sel,
    lin_part, lin_own, lin_block, own_terms, all_terms, low_part, low_in_parts, low_rows, eye, slot_terms, slot_other, slot_all,
    da_blocks, da_out, da_in, da_sum, a_over_out, a_over_in, b_over_out, b_over_in, low_kept,
    gs, gr, qs, qr, ws, wr, wl, ls, ss, sr,
):
    fs = lax.axis_index("fsdp")
    t = lax.axis_index("tp")
    k, c = fs // 2, fs % 2
    x, zh = k // 2, k % 2
    y, zl = t % 4, t // 4
    hid = h_ref.shape[1]
    feat = g_ref.shape[1]
    rank = a_ref.shape[0]
    chips = 8
    share = 2 * feat // chips

    widths = widths_of(hid)
    starts = [sum(widths[:p]) for p in range(len(widths))]

    def across(j):
        return {"fsdp": 2 * j + c, "tp": t}

    def along(tt):
        return {"fsdp": fs, "tp": tt}

    sibling = {"fsdp": 2 * k + 1 - c, "tp": t}

    def slot(b):
        return store[ids[b]]

    def send(src, dst, s_sem, r_sem, dev):
        return pltpu.make_async_remote_copy(
            src_ref=src, dst_ref=dst, send_sem=s_sem, recv_sem=r_sem,
            device_id=dev, device_id_type=MESH,
        )

    def others(me, body):
        def step(i, _):
            body(lax.rem(me + i, chips))
            return 0

        lax.fori_loop(1, chips, step, 0)

    def loop(n, body):
        def step(i, _):
            body(i)
            return 0

        lax.fori_loop(0, n, step, 0)

    def corner(j):
        xj = j // 2
        return ((xj + 1) // 2) % 2, xj // 2, j % 2

    here = corner(k)
    beside = (2 * (x + 1 - 2 * (x % 2)) + zh, 2 * (3 - x) + zh, 2 * x + 1 - zh)
    orders = ((0, 1, 2), (1, 2, 0), (2, 0, 1), (0, 2, 1), (1, 0, 2), (1, 2, 0))

    def apart(j, p):
        there = corner(j)
        return [(here[d] + there[d]) % 2 for d in orders[p]]

    mine = pl.ds(pl.multiple_of(c * feat, feat), feat)

    def b_cols(xx):
        return pl.ds(pl.multiple_of(xx * 4 * feat, 4 * feat), 4 * feat)

    load_g = pltpu.make_async_copy(g_ref, g_in, ls.at[0])
    load_h = pltpu.make_async_copy(h_ref, h_in, ls.at[1])
    load_a = pltpu.make_async_copy(a_ref, a_all.at[c, x], ls.at[2])
    load_b = pltpu.make_async_copy(b_ref.at[:, b_cols(x)], b_all.at[c, x], ls.at[3])

    load_g.start()
    corners = [lax.broadcasted_iota(jnp.int32, (BLOCK, BLOCK), d) for d in range(2)]
    eye[...] = (corners[0] == corners[1]).astype(f32)

    barrier = pltpu.get_barrier_semaphore()
    pl.semaphore_signal(barrier, inc=1, device_id=sibling, device_id_type=MESH)
    others(k, lambda j: pl.semaphore_signal(barrier, inc=1, device_id=across(j), device_id_type=MESH))
    others(t, lambda j: pl.semaphore_signal(barrier, inc=1, device_id=along(j), device_id_type=MESH))

    def w_rows(p):
        return pl.ds(starts[p], widths[p])

    def w_here(p):
        return pltpu.make_async_copy(w_ref.at[w_rows(p)], w_all.at[w_rows(p), mine], wl.at[p])

    def w_out(p):
        return send(w_ref.at[w_rows(p)], w_all.at[w_rows(p), mine], ws.at[p], wr.at[p], sibling)

    for p in range(len(widths)):
        w_here(p).start()

    for cp in (load_b, load_a, load_h):
        cp.start()
    load_g.wait()

    def masked(j):
        rows = lax.broadcasted_iota(jnp.int32, (BLOCK, feat), 0)
        g = g_in[pl.ds(pl.multiple_of(j * BLOCK, BLOCK), BLOCK), :]
        return jnp.where(rows < live[2 * t + j], g, jnp.zeros((), bf16))

    dy[y, zl, :, mine] = masked(c)
    stage[...] = masked(1 - c)
    pl.semaphore_wait(barrier, 15)

    to_sib = send(stage, dy.at[y, zl, :, mine], ss.at[0], sr.at[0], sibling)
    to_sib.start()
    for p in range(len(widths)):
        w_out(p).start()
    to_sib.wait_recv()

    y_next, y_prev, y_far = lax.rem(y + 1, 4), lax.rem(y + 3, 4), lax.rem(y + 2, 4)

    def dy_send(yy, zz, n, tt):
        return send(dy.at[yy, zz], dy.at[yy, zz], gs.at[0, n], gr.at[0, zz * 4 + yy], along(tt))

    def dy_half(yy, zz, half, tt):
        rows = pl.ds(half * (BLOCK // 2), BLOCK // 2)
        piece = dy.at[yy, zz, rows]
        return send(piece, piece, gs.at[1, half * 2 + zz], gr.at[1 + half, zz * 4 + yy], along(tt))

    def dy_wait(yy, zz):
        send(dy.at[yy, zz], dy.at[yy, zz], gs.at[0, 0], gr.at[0, zz * 4 + yy], sibling).wait_recv()

    own = [dy_send(y, zl, 0, (1 - zl) * 4 + y)]
    own += [dy_send(y, zl, 1 + i, zl * 4 + yy) for i, yy in enumerate((y_next, y_prev))]
    for cp in own:
        cp.start()

    def a_copy(xx):
        return send(a_ref, a_all.at[c, x], gs.at[2, xx], gr.at[3, x], across(2 * xx + zh))

    def b_copy(xx):
        return send(b_ref.at[:, b_cols(xx)], b_all.at[c, x], gs.at[3, xx], gr.at[4, x], across(2 * xx + zh))

    def others_x(body):
        for n in range(1, 4):
            body(lax.rem(x + n, 4))

    others_x(lambda xx: a_copy(xx).start())
    others_x(lambda xx: b_copy(xx).start())

    relay = [dy_send(y, 1 - zl, 3 + i, zl * 4 + yy) for i, yy in enumerate((y_next, y_prev))]

    def take_z():
        dy_wait(y, 1 - zl)
        for cp in relay:
            cp.start()
        take_near(zl)

    partner = across(2 * x + 1 - zh)
    a_fwd = send(a_all.at[c], a_all.at[c], ss.at[1], sr.at[1], sibling)
    b_fwd = send(b_all.at[c], b_all.at[c], ss.at[2], sr.at[2], sibling)
    a_over = send(a_over_out, a_over_in, ss.at[7], sr.at[7], partner)
    b_over = send(b_over_out, b_over_in, ss.at[8], sr.at[8], partner)

    def y_of(s):
        return lax.rem(y + s + (s // 2) * (5 - 2 * s), 4)

    def pieces(p):
        return 8 * widths[p] // 128

    def q_send(p, j, at, d):
        run = pl.ds(0, pieces(p) + 1)
        return send(out_q.at[p, j, run], in_q.at[p, at, run], qs.at[p, j], qr.at[p, at], across(beside[d]))

    def cols(p, n):
        return pl.ds(pl.multiple_of(starts[p] + n * TILE, TILE), TILE)

    def inner(n):
        return pl.ds(pl.multiple_of(n * TILE, TILE), TILE)

    def code_and_send(s, zz, p, j, at, d):
        rows = pl.ds(pl.multiple_of(zz * BLOCK, BLOCK), BLOCK)

        def top(n, peak):
            v = jnp.abs(part[s, rows, cols(p, n)])
            return jnp.maximum(peak, jnp.maximum(v[:, :128], v[:, 128:]))

        peak = lax.fori_loop(0, widths[p] // TILE, top, jnp.zeros((BLOCK, 128), f32))
        level = level_of(jnp.max(peak, axis=1, keepdims=True))
        gain = TOP * jnp.exp(level * (-1.0 / STEPS))

        marks = jnp.sum(eye[...] * level, axis=0, keepdims=True)
        out_q[p, j, pieces(p)] = jnp.broadcast_to(marks, (16, BLOCK)).astype(jnp.int32).astype(jnp.int16)

        def code(n):
            q = jnp.round(part[s, rows, cols(p, n)] * gain).astype(jnp.int32).astype(jnp.int16)
            for i in range(TILE // 128):
                out_q[p, j, pl.ds(n * 16 + 8 * i, 8)] = q[:, 128 * i : 128 * i + 128].reshape(8, 16, 128)

        loop(widths[p] // TILE, code)
        q_send(p, j, at, d).start()

    def fold(s, zz, p, at, last):
        q_send(p, 0, at, 0).wait_recv()
        level = jnp.sum(eye[...] * in_q[p, at, pieces(p)].astype(f32)[:1], axis=1, keepdims=True)
        scale = jnp.broadcast_to(jnp.exp(level * (1.0 / STEPS)) * (1.0 / TOP), (BLOCK, 128))
        rows = pl.ds(pl.multiple_of(zz * BLOCK, BLOCK), BLOCK)

        def add(n):
            q = [in_q[p, at, pl.ds(n * 16 + 8 * i, 8)].astype(f32).reshape(BLOCK, 128) for i in range(TILE // 128)]
            v = part[s, rows, cols(p, n)] + jnp.concatenate([u * scale for u in q], axis=1)
            if last:
                v = v + nn(low_rows[...], a_sel[:, cols(p, n)])
                o_h[:, cols(p, n)] = v.astype(bf16)
            else:
                part[s, rows, cols(p, n)] = v

        loop(widths[p] // TILE, add)

    def stage1(s):
        yy = y_of(s)
        for p in range(len(widths)):
            at = w_rows(p)
            part[s, :, at] = nt(dy[yy].reshape(2 * BLOCK, 2 * feat), w_all[at, :])
            for zz in range(2):
                j = zz * 4 + yy
                r1, r2, r3 = apart(j, p)

                @pl.when(r1 == 1)
                def _():
                    code_and_send(s, zz, p, j, r2 * 2 + r3, orders[p][0])

    def stage1_alone(i):
        zz = lax.rem(zl + i, 2)
        j = zz * 4 + y
        rows = pl.ds(pl.multiple_of(zz * BLOCK, BLOCK), BLOCK)

        @pl.when(i == 1)
        def _():
            take_z()

        for p in range(len(widths)):
            @pl.when(i == 0)
            def _():
                w_here(p).wait()
                w_out(p).wait_recv()

            at = w_rows(p)
            part[0, rows, at] = nt(dy[y, zz], w_all[at, :])
            r1, r2, r3 = apart(j, p)

            @pl.when(r1 == 1)
            def _():
                code_and_send(0, zz, p, j, r2 * 2 + r3, orders[p][0])

    def stage2(s):
        yy = y_of(s)
        for p in range(len(widths)):
            for zz in range(2):
                j = zz * 4 + yy
                r1, r2, r3 = apart(j, p)

                @pl.when(r1 == 0)
                def _():
                    fold(s, zz, p, r2 * 2 + r3, False)

                    @pl.when(r2 == 1)
                    def _():
                        code_and_send(s, zz, p, j, 4 + r3, orders[p][1])

    def stage3(s):
        yy = y_of(s)
        for p in range(len(widths)):
            for zz in range(2):
                j = zz * 4 + yy
                r1, r2, r3 = apart(j, p)

                @pl.when(r1 + r2 == 0)
                def _():
                    fold(s, zz, p, 4 + r3, False)

                    @pl.when(r3 == 1)
                    def _():
                        code_and_send(s, zz, p, j, 6, orders[p][2])

    def stage4(s):
        yy = y_of(s)
        for p in range(len(widths)):
            for zz in range(2):
                @pl.when(zz * 4 + yy == k)
                def _():
                    fold(s, zz, p, 6, True)

    def lin_copy(j):
        return send(lin_part.at[t], lin_part.at[t], gs.at[4, j], gr.at[5, t], along(j))

    def lin_block_copy(j):
        return send(lin_own, lin_block, gs.at[5, j], sr.at[6], across(j))

    low_out_copy = send(low_part, low_in_parts.at[k], ss.at[5], gr.at[7, k], across(t))

    def low_copy(tt):
        return send(low_kept, low_kept, gs.at[6, tt], sr.at[5], along(tt))

    def da_copy(xx):
        return send(da_out.at[xx], da_in.at[x], gs.at[7, xx], gr.at[8, x], across(2 * xx + zh))

    da_sib = send(da_blocks.at[0], da_blocks.at[1], ss.at[4], sr.at[4], sibling)
    da_over = send(da_blocks.at[0], da_blocks.at[2], ss.at[9], sr.at[9], partner)
    da_sib_over = send(da_blocks.at[2], da_blocks.at[3], ss.at[10], sr.at[10], sibling)

    def ob_copy(j):
        return send(slot_terms.at[c, j], slot_all.at[t, k], gs.at[8, j], gr.at[9, k], across(j))

    def ob_along(tt, n, to):
        return send(slot_all.at[tt], slot_all.at[tt], gs.at[9, n], gr.at[10, tt], along(to))

    def ob_wait(tt):
        send(slot_all.at[tt], slot_all.at[tt], gs.at[9, 0], gr.at[10, tt], sibling).wait_recv()

    slot_swap = send(slot_terms.at[1 - c], slot_other, ss.at[3], sr.at[3], sibling)
    ob_own = [ob_along(t, 0, (1 - zl) * 4 + y)]
    ob_own += [ob_along(t, 1 + i, zl * 4 + yy) for i, yy in enumerate((y_next, y_prev, y_far))]
    t_z = (1 - zl) * 4 + y
    ob_relay = [ob_along(t_z, 4 + i, zl * 4 + yy) for i, yy in enumerate((y_next, y_prev, y_far))]
    halves = [dy_half(y_next, zz, 0, zl * 4 + y_prev) for zz in range(2)]
    halves += [dy_half(y_prev, zz, 1, zl * 4 + y_next) for zz in range(2)]

    def take_near(zz):
        dy_wait(y_next, zz)
        dy_half(y_next, zz, 0, zl * 4 + y_prev).start()
        dy_wait(y_prev, zz)
        dy_half(y_prev, zz, 1, zl * 4 + y_next).start()

    def take_near_second():
        take_near(1 - zl)

    def take_far():
        for zz in (zl, 1 - zl):
            for side in range(2):
                dy_half(y_far, zz, side, zl * 4 + y_next).wait_recv()

    def share_adapters():
        others_x(lambda xx: send(a_ref, a_all.at[c, xx], gs.at[2, xx], gr.at[3, xx], sibling).wait_recv())
        load_a.wait()
        a_fwd.start()
        others_x(lambda xx: send(b_ref.at[:, b_cols(0)], b_all.at[c, xx], gs.at[3, xx], gr.at[4, xx], sibling).wait_recv())
        load_b.wait()
        b_fwd.start()

    def features(z):
        return pl.ds(pl.multiple_of(z * 2 * feat, 2 * feat), 2 * feat)

    def hand_over():
        a_fwd.wait_recv()
        s = slot(2 * (2 * x + 1 - zh) + c)
        a_over_out[...] = a_all[s % 2, s // 4]
        a_over.start()
        b_fwd.wait_recv()
        s = slot(2 * t + c)
        b_over_out[...] = b_all[s % 2, s // 4, :, features(1 - zh)]
        b_over.start()

    def low_activations():
        s = slot(fs)
        a_over.wait_recv()
        here_too = ((s // 2) % 2 == zh).astype(f32).astype(bf16)
        there = ((s // 2) % 2 != zh).astype(f32).astype(bf16)
        a_sel[...] = a_all[s % 2, s // 4] * here_too + a_over_in[...] * there
        load_h.wait()
        lin_part[t] = nt(a_sel[...], h_in[...])
        others(t, lambda j: lin_copy(j).start())

    def share_low_activations():
        others(t, lambda j: send(lin_part.at[j], lin_part.at[j], gs.at[4, j], gr.at[5, j], along(j)).wait_recv())
        total = lin_part[0]
        for j in range(1, chips):
            total = total + lin_part[j]
        lin_own[...] = (adapter_scale * total).astype(bf16)

        @pl.when(k == t)
        def _():
            others(k, lambda j: lin_block_copy(j).start())

    def low_cotangents():
        s = slot(2 * t + c)
        b_over.wait_recv()
        here_too = ((s // 2) % 2 == zh).astype(f32).astype(bf16)
        there = ((s // 2) % 2 != zh).astype(f32).astype(bf16)
        b_sel = b_all[s % 2, s // 4, :, features(zh)] * here_too + b_over_in[...] * there
        low_part[...] = nt(b_sel, dy[y, zl])

        @pl.when(k != t)
        def _():
            low_out_copy.start()

    def low_sum():
        @pl.when(k == t)
        def _():
            low_in_parts[k] = low_part[...]
            others(k, lambda j: send(low_part, low_in_parts.at[j], ss.at[5], gr.at[7, j], across(j)).wait_recv())
            total = low_in_parts[0]
            for j in range(1, chips):
                total = total + low_in_parts[j]
            low_kept[...] = (adapter_scale * total).astype(bf16)
            others(t, lambda j: low_copy(j).start())

    def output_map_terms():
        @pl.when(k != t)
        def _():
            send(lin_own, lin_block, ss.at[6], sr.at[6], across(t)).wait_recv()

        @pl.when(k == t)
        def _():
            lin_block[...] = lin_own[...]

        for n in range(chips):
            own_terms[n] = nn(lin_block[...], dy[y, zl, :, n * share : (n + 1) * share])
        others(t, lambda j: terms_copy(j).start())
        all_terms[t] = own_terms[t]

    def terms_copy(j):
        return send(own_terms.at[j], all_terms.at[t], gs.at[10, j], gr.at[6, t], along(j))

    def output_map_slots():
        others(t, lambda j: send(own_terms.at[j], all_terms.at[j], gs.at[10, j], gr.at[6, j], along(j)).wait_recv())
        slots = [slot(2 * j + c) for j in range(chips)]

        def one(n):
            s = 2 * lax.rem(n, chips) + n // chips
            out = jnp.zeros((rank, share), f32)
            for j in range(chips):
                out = out + all_terms[j] * (slots[j] == s).astype(f32)
            slot_terms[n // chips, lax.rem(n, chips)] = out

        loop(2 * chips, one)
        slot_swap.start()

    def output_map_sums():
        slot_swap.wait_recv()
        slot_terms[c] = slot_terms[c] + slot_other[...]
        others(k, lambda j: ob_copy(j).start())
        slot_all[t, k] = slot_terms[c, k]

    def output_map_share():
        others(k, lambda j: send(slot_terms.at[c, j], slot_all.at[t, j], gs.at[8, j], gr.at[9, j], across(j)).wait_recv())
        for cp in ob_own:
            cp.start()

    def output_map_relay():
        ob_wait(t_z)
        for cp in ob_relay:
            cp.start()

    def input_map_terms():
        @pl.when(k != t)
        def _():
            low_copy(k).wait_recv()

        low = low_kept[...]
        low_rows[...] = low.astype(f32).T.astype(bf16)
        da_code(nn(low, h_in[...]), da_blocks.at[0])
        da_sib.start()
        da_over.start()

    def da_code(v, ref):
        level = level_of(jnp.max(jnp.abs(v), axis=1, keepdims=True))
        gain = TOP * jnp.exp(level * (-1.0 / STEPS))
        ref[:, :hid] = jnp.round(v * gain).astype(jnp.int32).astype(jnp.int16)
        ref[:, hid:] = jnp.broadcast_to(level, (rank, 128)).astype(jnp.int32).astype(jnp.int16)

    def da_value(ref, gain):
        scale = jnp.exp(ref[:, hid:].astype(f32) * (1.0 / STEPS))[:, :1] * (gain * (1.0 / TOP))
        return ref[:, :hid].astype(f32) * scale

    def input_map_pass():
        da_over.wait_recv()
        da_sib_over.start()

    def input_map_sums():
        da_sib.wait_recv()
        da_sib_over.wait_recv()
        k_z = 2 * x + 1 - zh
        slots = [slot(b) for b in (fs, 2 * k + 1 - c, 2 * k_z + c, 2 * k_z + 1 - c)]

        def one(n):
            xx = lax.rem(x + n, 4)
            out = jnp.zeros((rank, hid), f32)
            for i in range(4):
                out = out + da_value(da_blocks.at[i], (slots[i] == 2 * (2 * xx + zh) + c).astype(f32))

            @pl.when(n == 0)
            def _():
                da_sum[...] = out

            @pl.when(n > 0)
            def _():
                da_code(out, da_out.at[xx])
                da_copy(xx).start()

        loop(4, one)

    def input_map_end():
        def one(n):
            xx = lax.rem(x + n, 4)
            send(da_out.at[xx], da_in.at[xx], gs.at[7, xx], gr.at[8, xx], sibling).wait_recv()
            da_sum[...] += da_value(da_in.at[xx], 1.0)
            return 0

        lax.fori_loop(1, 4, lambda n, _: one(n), 0)
        o_a[...] = da_sum[...]

    plan = {
        1: ((share_adapters, hand_over, low_activations, low_cotangents, take_near_second), (share_low_activations, low_sum), (), ()),
        2: ((), (output_map_terms, input_map_terms), (), (output_map_slots, input_map_pass)),
        3: ((output_map_sums, take_far), (input_map_sums,), (output_map_share,), ()),
        4: ((), (), (output_map_relay,), ()),
    }

    def when(cond, body):
        pl.when(cond)(body)

    def run(it, place):
        for i, spots in plan.items():
            if spots[place]:
                when(it == i, lambda: [f() for f in spots[place]] and None)

    def step(i):
        it = i + 1
        run(it, 0)
        when(it < 4, lambda: stage1(it))
        run(it, 1)
        when(it < 5, lambda: stage2(it - 1))
        run(it, 2)
        when((it >= 2) & (it < 6), lambda: stage3(it - 2))
        when(it >= 3, lambda: stage4(it - 3))
        run(it, 3)

    loop(2, stage1_alone)
    loop(6, step)

    input_map_end()
    others(t, lambda j: pl.when(j != t_z)(lambda: ob_wait(j)))

    def put(i):
        tt, j = i % chips, i // chips
        o_b[:, pl.ds(pl.multiple_of(i * share, share), share)] = slot_all[tt, j]

    loop(chips * chips, put)

    for cp in (to_sib, a_fwd, b_fwd, a_over, b_over, slot_swap, da_sib, da_over, da_sib_over, *own, *relay, *halves, *ob_own, *ob_relay):
        cp.wait_send()
    for p in range(len(widths)):
        w_out(p).wait_send()
        others(k, lambda j: q_send(p, j, 0, 0).wait_send())
    for copy in (a_copy, b_copy, da_copy):
        others_x(lambda xx: copy(xx).wait_send())
    others(k, lambda j: ob_copy(j).wait_send())
    others(t, lambda j: lin_copy(j).wait_send())
    others(t, lambda j: terms_copy(j).wait_send())

    @pl.when(k == t)
    def _():
        others(t, lambda j: low_copy(j).wait_send())
        others(k, lambda j: lin_block_copy(j).wait_send())

    @pl.when(k != t)
    def _():
        low_out_copy.wait_send()


def local(h, g, w, a, b, ids, live, store):
    tok, hid = h.shape
    feat = g.shape[1]
    rank = a.shape[2]
    wide = b.shape[2]
    chips = 8
    share = 2 * feat // chips
    widths = widths_of(hid)
    a_t = jnp.swapaxes(a, 1, 2).reshape(rank, hid)
    vm = pl.BlockSpec(memory_space=pltpu.VMEM)
    sm = pl.BlockSpec(memory_space=pltpu.SMEM)
    far = pl.BlockSpec(memory_space=pl.ANY)
    dma = pltpu.SemaphoreType.DMA
    o_h, o_a, o_b = pl.pallas_call(
        kernel,
        out_shape=(
            jax.ShapeDtypeStruct((tok, hid), bf16),
            jax.ShapeDtypeStruct((rank, hid), f32),
            jax.ShapeDtypeStruct((rank, wide), f32),
        ),
        in_specs=[sm, sm, sm] + [far] * 5,
        out_specs=(vm, vm, vm),
        scratch_shapes=[
            pltpu.VMEM((hid, 2 * feat), bf16),
            pltpu.VMEM((4, 2, BLOCK, 2 * feat), bf16),
            pltpu.VMEM((BLOCK, feat), bf16),
            pltpu.VMEM((4, 2 * BLOCK, hid), f32),
            pltpu.VMEM((6, chips, max(widths) // 16 + 1, 16, 128), jnp.int16),
            pltpu.VMEM((6, chips - 1, max(widths) // 16 + 1, 16, 128), jnp.int16),
            pltpu.VMEM((BLOCK, hid), bf16),
            pltpu.VMEM((2 * BLOCK, feat), bf16),
            pltpu.VMEM((2, 4, rank, hid), bf16),
            pltpu.VMEM((2, 4, rank, 4 * feat), bf16),
            pltpu.VMEM((rank, hid), bf16),
            pltpu.VMEM((chips, rank, BLOCK), f32),
            pltpu.VMEM((rank, BLOCK), bf16),
            pltpu.VMEM((rank, BLOCK), bf16),
            pltpu.VMEM((chips, rank, share), f32),
            pltpu.VMEM((chips, rank, share), f32),
            pltpu.VMEM((rank, BLOCK), f32),
            pltpu.VMEM((chips, rank, BLOCK), f32),
            pltpu.VMEM((BLOCK, rank), bf16),
            pltpu.VMEM((BLOCK, BLOCK), f32),
            pltpu.VMEM((2, chips, rank, share), f32),
            pltpu.VMEM((chips, rank, share), f32),
            pltpu.VMEM((chips, chips, rank, share), f32),
            pltpu.VMEM((4, rank, hid + 128), jnp.int16),
            pltpu.VMEM((4, rank, hid + 128), jnp.int16),
            pltpu.VMEM((4, rank, hid + 128), jnp.int16),
            pltpu.VMEM((rank, hid), f32),
            pltpu.VMEM((rank, hid), bf16),
            pltpu.VMEM((rank, hid), bf16),
            pltpu.VMEM((rank, 2 * feat), bf16),
            pltpu.VMEM((rank, 2 * feat), bf16),
            pltpu.VMEM((rank, BLOCK), bf16),
            dma((11, 8)),
            dma((11, 8)),
            dma((6, 8)),
            dma((6, 7)),
            dma((6,)),
            dma((6,)),
            dma((6,)),
            dma((4,)),
            dma((11,)),
            dma((11,)),
        ],
        compiler_params=pltpu.CompilerParams(
            collective_id=0, has_side_effects=True, vmem_limit_bytes=62 << 20
        ),
    )(ids, live, store, h, g, w, a_t, b.reshape(rank, wide))
    o_h, o_a, o_b = pl.pallas_call(
        keep,
        out_shape=tuple(jax.ShapeDtypeStruct(o.shape, o.dtype) for o in (o_h, o_a, o_b)),
        in_specs=[far] * 3,
        out_specs=(far,) * 3,
        scratch_shapes=[pltpu.VMEM(o.shape, o.dtype) for o in (o_h, o_a, o_b)] + [dma((3,)), dma((3,))],
        compiler_params=pltpu.CompilerParams(vmem_limit_bytes=62 << 20),
    )(o_h, o_a, o_b)
    return (
        o_h,
        jnp.swapaxes(o_a.reshape(1, rank, hid), 1, 2),
        o_b.reshape(1, rank, wide),
    )


def solution(mesh):
    placed = (
        P("fsdp", "tp"),
        P("tp", "fsdp"),
        P("tp", "fsdp"),
        P("fsdp", "tp", None),
        P("fsdp", None, None),
        P(),
        P(),
        P(),
    )
    return jax.shard_map(
        local,
        mesh=mesh,
        in_specs=placed,
        out_specs=(P("fsdp", "tp"), P("fsdp", "tp", None), P("fsdp", None, None)),
        check_vma=False,
    )
```

```python
import functools
import math

import jax
import jax.numpy as jnp
from jax import lax
from jax.experimental import pallas as pl
from jax.experimental.pallas import tpu as pltpu
from jax.sharding import PartitionSpec as P

BLOCK = 128
TILE = 256
MESH = pl.DeviceIdType.MESH
adapter_scale = 2.0
f32 = jnp.float32
bf16 = jnp.bfloat16

TOP = 32000.0
STEPS = 8.0 / math.log(2.0)


def nt(a, b):
    return lax.dot_general(a, b, (((1,), (1,)), ((), ())), preferred_element_type=f32)


def nn(a, b):
    return lax.dot_general(a, b, (((1,), (0,)), ((), ())), preferred_element_type=f32)


def level_of(peak):
    return jnp.ceil(jnp.log(jnp.maximum(peak, 1e-30)) * STEPS)


def widths_of(hid):
    tiles = hid // TILE
    return [(tiles * (p + 1) // 6 - tiles * p // 6) * TILE for p in range(6)][::-1]


def keep(h, a, b, o_h, o_a, o_b, v_h, v_a, v_b, came, left):
    ways = ((h, v_h, o_h), (b, v_b, o_b), (a, v_a, o_a))
    into = [pltpu.make_async_copy(x, v, came.at[i]) for i, (x, v, _) in enumerate(ways)]
    out = [pltpu.make_async_copy(v, o, left.at[i]) for i, (_, v, o) in enumerate(ways)]
    for cp in into:
        cp.start()
    for first, second in zip(into, out):
        first.wait()
        second.start()
    for cp in out:
        cp.wait()


def kernel(
    ids, live, store, h_ref, g_ref, w_ref, a_ref, b_ref,
    o_h, o_a, o_b,
    w_all, dy, stage, part, out_q, in_q, h_in, g_in, a_all, b_all, a_sel,
    lin_part, lin_own, lin_block, own_terms, all_terms, low_part, low_in_parts, low_rows, eye, slot_terms, slot_other, slot_all,
    da_blocks, da_out, da_in, da_sum, a_over_out, a_over_in, b_over_out, b_over_in, low_kept,
    gs, gr, qs, qr, ws, wr, wl, ls, ss, sr,
):
    fs = lax.axis_index("fsdp")
    t = lax.axis_index("tp")
    k, c = fs // 2, fs % 2
    x, zh = k // 2, k % 2
    y, zl = t % 4, t // 4
    hid = h_ref.shape[1]
    feat = g_ref.shape[1]
    rank = a_ref.shape[0]
    chips = 8
    share = 2 * feat // chips

    widths = widths_of(hid)
    starts = [sum(widths[:p]) for p in range(len(widths))]

    def across(j):
        return {"fsdp": 2 * j + c, "tp": t}

    def along(tt):
        return {"fsdp": fs, "tp": tt}

    sibling = {"fsdp": 2 * k + 1 - c, "tp": t}

    def slot(b):
        return store[ids[b]]

    def send(src, dst, s_sem, r_sem, dev):
        return pltpu.make_async_remote_copy(
            src_ref=src, dst_ref=dst, send_sem=s_sem, recv_sem=r_sem,
            device_id=dev, device_id_type=MESH,
        )

    def others(me, body):
        def step(i, _):
            body(lax.rem(me + i, chips))
            return 0

        lax.fori_loop(1, chips, step, 0)

    def loop(n, body):
        def step(i, _):
            body(i)
            return 0

        lax.fori_loop(0, n, step, 0)

    def corner(j):
        xj = j // 2
        return ((xj + 1) // 2) % 2, xj // 2, j % 2

    here = corner(k)
    beside = (2 * (x + 1 - 2 * (x % 2)) + zh, 2 * (3 - x) + zh, 2 * x + 1 - zh)
    orders = ((0, 1, 2), (1, 2, 0), (2, 0, 1), (0, 2, 1), (1, 0, 2), (1, 2, 0))

    def apart(j, p):
        there = corner(j)
        return [(here[d] + there[d]) % 2 for d in orders[p]]

    mine = pl.ds(pl.multiple_of(c * feat, feat), feat)

    def b_cols(xx):
        return pl.ds(pl.multiple_of(xx * 4 * feat, 4 * feat), 4 * feat)

    load_g = pltpu.make_async_copy(g_ref, g_in, ls.at[0])
    load_h = pltpu.make_async_copy(h_ref, h_in, ls.at[1])
    load_a = pltpu.make_async_copy(a_ref, a_all.at[c, x], ls.at[2])
    load_b = pltpu.make_async_copy(b_ref.at[:, b_cols(x)], b_all.at[c, x], ls.at[3])

    load_g.start()
    corners = [lax.broadcasted_iota(jnp.int32, (BLOCK, BLOCK), d) for d in range(2)]
    eye[...] = (corners[0] == corners[1]).astype(f32)

    barrier = pltpu.get_barrier_semaphore()
    pl.semaphore_signal(barrier, inc=1, device_id=sibling, device_id_type=MESH)
    others(k, lambda j: pl.semaphore_signal(barrier, inc=1, device_id=across(j), device_id_type=MESH))
    others(t, lambda j: pl.semaphore_signal(barrier, inc=1, device_id=along(j), device_id_type=MESH))

    def w_rows(p):
        return pl.ds(starts[p], widths[p])

    def w_here(p):
        return pltpu.make_async_copy(w_ref.at[w_rows(p)], w_all.at[w_rows(p), mine], wl.at[p])

    def w_out(p):
        return send(w_ref.at[w_rows(p)], w_all.at[w_rows(p), mine], ws.at[p], wr.at[p], sibling)

    for p in range(len(widths)):
        w_here(p).start()

    for cp in (load_b, load_a, load_h):
        cp.start()
    load_g.wait()

    def masked(j):
        rows = lax.broadcasted_iota(jnp.int32, (BLOCK, feat), 0)
        g = g_in[pl.ds(pl.multiple_of(j * BLOCK, BLOCK), BLOCK), :]
        return jnp.where(rows < live[2 * t + j], g, jnp.zeros((), bf16))

    dy[y, zl, :, mine] = masked(c)
    stage[...] = masked(1 - c)
    pl.semaphore_wait(barrier, 15)

    to_sib = send(stage, dy.at[y, zl, :, mine], ss.at[0], sr.at[0], sibling)
    to_sib.start()
    for p in range(len(widths)):
        w_out(p).start()
    to_sib.wait_recv()

    y_next, y_prev, y_far = lax.rem(y + 1, 4), lax.rem(y + 3, 4), lax.rem(y + 2, 4)

    def dy_send(yy, zz, n, tt):
        return send(dy.at[yy, zz], dy.at[yy, zz], gs.at[0, n], gr.at[0, zz * 4 + yy], along(tt))

    def dy_half(yy, zz, half, tt):
        rows = pl.ds(half * (BLOCK // 2), BLOCK // 2)
        piece = dy.at[yy, zz, rows]
        return send(piece, piece, gs.at[1, half * 2 + zz], gr.at[1 + half, zz * 4 + yy], along(tt))

    def dy_wait(yy, zz):
        send(dy.at[yy, zz], dy.at[yy, zz], gs.at[0, 0], gr.at[0, zz * 4 + yy], sibling).wait_recv()

    own = [dy_send(y, zl, 0, (1 - zl) * 4 + y)]
    own += [dy_send(y, zl, 1 + i, zl * 4 + yy) for i, yy in enumerate((y_next, y_prev))]
    for cp in own:
        cp.start()

    def a_copy(xx):
        return send(a_ref, a_all.at[c, x], gs.at[2, xx], gr.at[3, x], across(2 * xx + zh))

    def b_copy(xx):
        return send(b_ref.at[:, b_cols(xx)], b_all.at[c, x], gs.at[3, xx], gr.at[4, x], across(2 * xx + zh))

    def others_x(body):
        for n in range(1, 4):
            body(lax.rem(x + n, 4))

    others_x(lambda xx: a_copy(xx).start())
    others_x(lambda xx: b_copy(xx).start())

    relay = [dy_send(y, 1 - zl, 3 + i, zl * 4 + yy) for i, yy in enumerate((y_next, y_prev))]

    def take_z():
        dy_wait(y, 1 - zl)
        for cp in relay:
            cp.start()
        take_near(zl)

    partner = across(2 * x + 1 - zh)
    a_fwd = send(a_all.at[c], a_all.at[c], ss.at[1], sr.at[1], sibling)
    b_fwd = send(b_all.at[c], b_all.at[c], ss.at[2], sr.at[2], sibling)
    a_over = send(a_over_out, a_over_in, ss.at[7], sr.at[7], partner)
    b_over = send(b_over_out, b_over_in, ss.at[8], sr.at[8], partner)

    def y_of(s):
        return lax.rem(y + s + (s // 2) * (5 - 2 * s), 4)

    def pieces(p):
        return 8 * widths[p] // 128

    def q_send(p, j, at, d):
        run = pl.ds(0, pieces(p) + 1)
        return send(out_q.at[p, j, run], in_q.at[p, at, run], qs.at[p, j], qr.at[p, at], across(beside[d]))

    def cols(p, n):
        return pl.ds(pl.multiple_of(starts[p] + n * TILE, TILE), TILE)

    def inner(n):
        return pl.ds(pl.multiple_of(n * TILE, TILE), TILE)

    def code_and_send(s, zz, p, j, at, d):
        rows = pl.ds(pl.multiple_of(zz * BLOCK, BLOCK), BLOCK)

        def top(n, peak):
            v = jnp.abs(part[s, rows, cols(p, n)])
            return jnp.maximum(peak, jnp.maximum(v[:, :128], v[:, 128:]))

        peak = lax.fori_loop(0, widths[p] // TILE, top, jnp.zeros((BLOCK, 128), f32))
        level = level_of(jnp.max(peak, axis=1, keepdims=True))
        gain = TOP * jnp.exp(level * (-1.0 / STEPS))

        marks = jnp.sum(eye[...] * level, axis=0, keepdims=True)
        out_q[p, j, pieces(p)] = jnp.broadcast_to(marks, (16, BLOCK)).astype(jnp.int32).astype(jnp.int16)

        def code(n):
            q = jnp.round(part[s, rows, cols(p, n)] * gain).astype(jnp.int32).astype(jnp.int16)
            for i in range(TILE // 128):
                out_q[p, j, pl.ds(n * 16 + 8 * i, 8)] = q[:, 128 * i : 128 * i + 128].reshape(8, 16, 128)

        loop(widths[p] // TILE, code)
        q_send(p, j, at, d).start()

    def fold(s, zz, p, at, last):
        q_send(p, 0, at, 0).wait_recv()
        level = jnp.sum(eye[...] * in_q[p, at, pieces(p)].astype(f32)[:1], axis=1, keepdims=True)
        scale = jnp.broadcast_to(jnp.exp(level * (1.0 / STEPS)) * (1.0 / TOP), (BLOCK, 128))
        rows = pl.ds(pl.multiple_of(zz * BLOCK, BLOCK), BLOCK)

        def add(n):
            q = [in_q[p, at, pl.ds(n * 16 + 8 * i, 8)].astype(f32).reshape(BLOCK, 128) for i in range(TILE // 128)]
            v = part[s, rows, cols(p, n)] + jnp.concatenate([u * scale for u in q], axis=1)
            if last:
                v = v + nn(low_rows[...], a_sel[:, cols(p, n)])
                o_h[:, cols(p, n)] = v.astype(bf16)
            else:
                part[s, rows, cols(p, n)] = v

        loop(widths[p] // TILE, add)

    def stage1(s):
        yy = y_of(s)
        for p in range(len(widths)):
            at = w_rows(p)
            part[s, :, at] = nt(dy[yy].reshape(2 * BLOCK, 2 * feat), w_all[at, :])
            for zz in range(2):
                j = zz * 4 + yy
                r1, r2, r3 = apart(j, p)

                @pl.when(r1 == 1)
                def _():
                    code_and_send(s, zz, p, j, r2 * 2 + r3, orders[p][0])

    def stage1_alone(i):
        zz = lax.rem(zl + i, 2)
        j = zz * 4 + y
        rows = pl.ds(pl.multiple_of(zz * BLOCK, BLOCK), BLOCK)

        @pl.when(i == 1)
        def _():
            take_z()

        for p in range(len(widths)):
            @pl.when(i == 0)
            def _():
                w_here(p).wait()
                w_out(p).wait_recv()

            at = w_rows(p)
            part[0, rows, at] = nt(dy[y, zz], w_all[at, :])
            r1, r2, r3 = apart(j, p)

            @pl.when(r1 == 1)
            def _():
                code_and_send(0, zz, p, j, r2 * 2 + r3, orders[p][0])

    def stage2(s):
        yy = y_of(s)
        for p in range(len(widths)):
            for zz in range(2):
                j = zz * 4 + yy
                r1, r2, r3 = apart(j, p)

                @pl.when(r1 == 0)
                def _():
                    fold(s, zz, p, r2 * 2 + r3, False)

                    @pl.when(r2 == 1)
                    def _():
                        code_and_send(s, zz, p, j, 4 + r3, orders[p][1])

    def stage3(s):
        yy = y_of(s)
        for p in range(len(widths)):
            for zz in range(2):
                j = zz * 4 + yy
                r1, r2, r3 = apart(j, p)

                @pl.when(r1 + r2 == 0)
                def _():
                    fold(s, zz, p, 4 + r3, False)

                    @pl.when(r3 == 1)
                    def _():
                        code_and_send(s, zz, p, j, 6, orders[p][2])

    def stage4(s):
        yy = y_of(s)
        for p in range(len(widths)):
            for zz in range(2):
                @pl.when(zz * 4 + yy == k)
                def _():
                    fold(s, zz, p, 6, True)

    def lin_copy(j):
        return send(lin_part.at[t], lin_part.at[t], gs.at[4, j], gr.at[5, t], along(j))

    def lin_block_copy(j):
        return send(lin_own, lin_block, gs.at[5, j], sr.at[6], across(j))

    low_out_copy = send(low_part, low_in_parts.at[k], ss.at[5], gr.at[7, k], across(t))

    def low_copy(tt):
        return send(low_kept, low_kept, gs.at[6, tt], sr.at[5], along(tt))

    def da_copy(xx):
        return send(da_out.at[xx], da_in.at[x], gs.at[7, xx], gr.at[8, x], across(2 * xx + zh))

    da_sib = send(da_blocks.at[0], da_blocks.at[1], ss.at[4], sr.at[4], sibling)
    da_over = send(da_blocks.at[0], da_blocks.at[2], ss.at[9], sr.at[9], partner)
    da_sib_over = send(da_blocks.at[2], da_blocks.at[3], ss.at[10], sr.at[10], sibling)

    def ob_copy(j):
        return send(slot_terms.at[c, j], slot_all.at[t, k], gs.at[8, j], gr.at[9, k], across(j))

    def ob_along(tt, n, to):
        return send(slot_all.at[tt], slot_all.at[tt], gs.at[9, n], gr.at[10, tt], along(to))

    def ob_wait(tt):
        send(slot_all.at[tt], slot_all.at[tt], gs.at[9, 0], gr.at[10, tt], sibling).wait_recv()

    slot_swap = send(slot_terms.at[1 - c], slot_other, ss.at[3], sr.at[3], sibling)
    ob_own = [ob_along(t, 0, (1 - zl) * 4 + y)]
    ob_own += [ob_along(t, 1 + i, zl * 4 + yy) for i, yy in enumerate((y_next, y_prev, y_far))]
    t_z = (1 - zl) * 4 + y
    ob_relay = [ob_along(t_z, 4 + i, zl * 4 + yy) for i, yy in enumerate((y_next, y_prev, y_far))]
    halves = [dy_half(y_next, zz, 0, zl * 4 + y_prev) for zz in range(2)]
    halves += [dy_half(y_prev, zz, 1, zl * 4 + y_next) for zz in range(2)]

    def take_near(zz):
        dy_wait(y_next, zz)
        dy_half(y_next, zz, 0, zl * 4 + y_prev).start()
        dy_wait(y_prev, zz)
        dy_half(y_prev, zz, 1, zl * 4 + y_next).start()

    def take_near_second():
        take_near(1 - zl)

    def take_far():
        for zz in (zl, 1 - zl):
            for side in range(2):
                dy_half(y_far, zz, side, zl * 4 + y_next).wait_recv()

    def share_adapters():
        others_x(lambda xx: send(a_ref, a_all.at[c, xx], gs.at[2, xx], gr.at[3, xx], sibling).wait_recv())
        load_a.wait()
        a_fwd.start()
        others_x(lambda xx: send(b_ref.at[:, b_cols(0)], b_all.at[c, xx], gs.at[3, xx], gr.at[4, xx], sibling).wait_recv())
        load_b.wait()
        b_fwd.start()

    def features(z):
        return pl.ds(pl.multiple_of(z * 2 * feat, 2 * feat), 2 * feat)

    def hand_over():
        a_fwd.wait_recv()
        s = slot(2 * (2 * x + 1 - zh) + c)
        a_over_out[...] = a_all[s % 2, s // 4]
        a_over.start()
        b_fwd.wait_recv()
        s = slot(2 * t + c)
        b_over_out[...] = b_all[s % 2, s // 4, :, features(1 - zh)]
        b_over.start()

    def low_activations():
        s = slot(fs)
        a_over.wait_recv()
        here_too = ((s // 2) % 2 == zh).astype(f32).astype(bf16)
        there = ((s // 2) % 2 != zh).astype(f32).astype(bf16)
        a_sel[...] = a_all[s % 2, s // 4] * here_too + a_over_in[...] * there
        load_h.wait()
        lin_part[t] = nt(a_sel[...], h_in[...])
        others(t, lambda j: lin_copy(j).start())

    def share_low_activations():
        others(t, lambda j: send(lin_part.at[j], lin_part.at[j], gs.at[4, j], gr.at[5, j], along(j)).wait_recv())
        total = lin_part[0]
        for j in range(1, chips):
            total = total + lin_part[j]
        lin_own[...] = (adapter_scale * total).astype(bf16)

        @pl.when(k == t)
        def _():
            others(k, lambda j: lin_block_copy(j).start())

    def low_cotangents():
        s = slot(2 * t + c)
        b_over.wait_recv()
        here_too = ((s // 2) % 2 == zh).astype(f32).astype(bf16)
        there = ((s // 2) % 2 != zh).astype(f32).astype(bf16)
        b_sel = b_all[s % 2, s // 4, :, features(zh)] * here_too + b_over_in[...] * there
        low_part[...] = nt(b_sel, dy[y, zl])

        @pl.when(k != t)
        def _():
            low_out_copy.start()

    def low_sum():
        @pl.when(k == t)
        def _():
            low_in_parts[k] = low_part[...]
            others(k, lambda j: send(low_part, low_in_parts.at[j], ss.at[5], gr.at[7, j], across(j)).wait_recv())
            total = low_in_parts[0]
            for j in range(1, chips):
                total = total + low_in_parts[j]
            low_kept[...] = (adapter_scale * total).astype(bf16)
            others(t, lambda j: low_copy(j).start())

    def output_map_terms():
        @pl.when(k != t)
        def _():
            send(lin_own, lin_block, ss.at[6], sr.at[6], across(t)).wait_recv()

        @pl.when(k == t)
        def _():
            lin_block[...] = lin_own[...]

        for n in range(chips):
            own_terms[n] = nn(lin_block[...], dy[y, zl, :, n * share : (n + 1) * share])
        others(t, lambda j: terms_copy(j).start())
        all_terms[t] = own_terms[t]

    def terms_copy(j):
        return send(own_terms.at[j], all_terms.at[t], gs.at[10, j], gr.at[6, t], along(j))

    def output_map_slots():
        others(t, lambda j: send(own_terms.at[j], all_terms.at[j], gs.at[10, j], gr.at[6, j], along(j)).wait_recv())
        slots = [slot(2 * j + c) for j in range(chips)]

        def one(n):
            s = 2 * lax.rem(n, chips) + n // chips
            out = jnp.zeros((rank, share), f32)
            for j in range(chips):
                out = out + all_terms[j] * (slots[j] == s).astype(f32)
            slot_terms[n // chips, lax.rem(n, chips)] = out

        loop(2 * chips, one)
        slot_swap.start()

    def output_map_sums():
        slot_swap.wait_recv()
        slot_terms[c] = slot_terms[c] + slot_other[...]
        others(k, lambda j: ob_copy(j).start())
        slot_all[t, k] = slot_terms[c, k]

    def output_map_share():
        others(k, lambda j: send(slot_terms.at[c, j], slot_all.at[t, j], gs.at[8, j], gr.at[9, j], across(j)).wait_recv())
        for cp in ob_own:
            cp.start()

    def output_map_relay():
        ob_wait(t_z)
        for cp in ob_relay:
            cp.start()

    def input_map_terms():
        @pl.when(k != t)
        def _():
            low_copy(k).wait_recv()

        low = low_kept[...]
        low_rows[...] = low.astype(f32).T.astype(bf16)
        da_code(nn(low, h_in[...]), da_blocks.at[0])
        da_sib.start()
        da_over.start()

    def da_code(v, ref):
        level = level_of(jnp.max(jnp.abs(v), axis=1, keepdims=True))
        gain = TOP * jnp.exp(level * (-1.0 / STEPS))
        ref[:, :hid] = jnp.round(v * gain).astype(jnp.int32).astype(jnp.int16)
        ref[:, hid:] = jnp.broadcast_to(level, (rank, 128)).astype(jnp.int32).astype(jnp.int16)

    def da_value(ref, gain):
        scale = jnp.exp(ref[:, hid:].astype(f32) * (1.0 / STEPS))[:, :1] * (gain * (1.0 / TOP))
        return ref[:, :hid].astype(f32) * scale

    def input_map_pass():
        da_over.wait_recv()
        da_sib_over.start()

    def input_map_sums():
        da_sib.wait_recv()
        da_sib_over.wait_recv()
        k_z = 2 * x + 1 - zh
        slots = [slot(b) for b in (fs, 2 * k + 1 - c, 2 * k_z + c, 2 * k_z + 1 - c)]

        def one(n):
            xx = lax.rem(x + n, 4)
            out = jnp.zeros((rank, hid), f32)
            for i in range(4):
                out = out + da_value(da_blocks.at[i], (slots[i] == 2 * (2 * xx + zh) + c).astype(f32))

            @pl.when(n == 0)
            def _():
                da_sum[...] = out

            @pl.when(n > 0)
            def _():
                da_code(out, da_out.at[xx])
                da_copy(xx).start()

        loop(4, one)

    def input_map_end():
        def one(n):
            xx = lax.rem(x + n, 4)
            send(da_out.at[xx], da_in.at[xx], gs.at[7, xx], gr.at[8, xx], sibling).wait_recv()
            da_sum[...] += da_value(da_in.at[xx], 1.0)
            return 0

        lax.fori_loop(1, 4, lambda n, _: one(n), 0)
        o_a[...] = da_sum[...]

    def output_map_end():
        others(t, lambda j: pl.when(j != t_z)(lambda: ob_wait(j)))

        def put(i):
            tt, j = i % chips, i // chips
            o_b[:, pl.ds(pl.multiple_of(i * share, share), share)] = slot_all[tt, j]

        loop(chips * chips, put)

    plan = {
        1: ((share_adapters, hand_over, low_activations, low_cotangents, take_near_second), (share_low_activations, low_sum), (), ()),
        2: ((), (output_map_terms, input_map_terms), (), (output_map_slots, input_map_pass)),
        3: ((output_map_sums, take_far), (), (output_map_share,), ()),
        4: ((), (), (input_map_sums, output_map_relay), ()),
        6: ((input_map_end, output_map_end), (), (), ()),
    }

    def when(cond, body):
        pl.when(cond)(body)

    def run(it, place):
        for i, spots in plan.items():
            if spots[place]:
                when(it == i, lambda: [f() for f in spots[place]] and None)

    def step(i):
        it = i + 1
        run(it, 0)
        when(it < 4, lambda: stage1(it))
        run(it, 1)
        when(it < 5, lambda: stage2(it - 1))
        run(it, 2)
        when((it >= 2) & (it < 6), lambda: stage3(it - 2))
        when(it >= 3, lambda: stage4(it - 3))
        run(it, 3)

    loop(2, stage1_alone)
    loop(6, step)

    for cp in (to_sib, a_fwd, b_fwd, a_over, b_over, slot_swap, da_sib, da_over, da_sib_over, *own, *relay, *halves, *ob_own, *ob_relay):
        cp.wait_send()
    for p in range(len(widths)):
        w_out(p).wait_send()
        others(k, lambda j: q_send(p, j, 0, 0).wait_send())
    for copy in (a_copy, b_copy, da_copy):
        others_x(lambda xx: copy(xx).wait_send())
    others(k, lambda j: ob_copy(j).wait_send())
    others(t, lambda j: lin_copy(j).wait_send())
    others(t, lambda j: terms_copy(j).wait_send())

    @pl.when(k == t)
    def _():
        others(t, lambda j: low_copy(j).wait_send())
        others(k, lambda j: lin_block_copy(j).wait_send())

    @pl.when(k != t)
    def _():
        low_out_copy.wait_send()


def local(h, g, w, a, b, ids, live, store):
    tok, hid = h.shape
    feat = g.shape[1]
    rank = a.shape[2]
    wide = b.shape[2]
    chips = 8
    share = 2 * feat // chips
    widths = widths_of(hid)
    a_t = jnp.swapaxes(a, 1, 2).reshape(rank, hid)
    vm = pl.BlockSpec(memory_space=pltpu.VMEM)
    sm = pl.BlockSpec(memory_space=pltpu.SMEM)
    far = pl.BlockSpec(memory_space=pl.ANY)
    dma = pltpu.SemaphoreType.DMA
    o_h, o_a, o_b = pl.pallas_call(
        kernel,
        out_shape=(
            jax.ShapeDtypeStruct((tok, hid), bf16),
            jax.ShapeDtypeStruct((rank, hid), f32),
            jax.ShapeDtypeStruct((rank, wide), f32),
        ),
        in_specs=[sm, sm, sm] + [far] * 5,
        out_specs=(vm, vm, vm),
        scratch_shapes=[
            pltpu.VMEM((hid, 2 * feat), bf16),
            pltpu.VMEM((4, 2, BLOCK, 2 * feat), bf16),
            pltpu.VMEM((BLOCK, feat), bf16),
            pltpu.VMEM((4, 2 * BLOCK, hid), f32),
            pltpu.VMEM((6, chips, max(widths) // 16 + 1, 16, 128), jnp.int16),
            pltpu.VMEM((6, chips - 1, max(widths) // 16 + 1, 16, 128), jnp.int16),
            pltpu.VMEM((BLOCK, hid), bf16),
            pltpu.VMEM((2 * BLOCK, feat), bf16),
            pltpu.VMEM((2, 4, rank, hid), bf16),
            pltpu.VMEM((2, 4, rank, 4 * feat), bf16),
            pltpu.VMEM((rank, hid), bf16),
            pltpu.VMEM((chips, rank, BLOCK), f32),
            pltpu.VMEM((rank, BLOCK), bf16),
            pltpu.VMEM((rank, BLOCK), bf16),
            pltpu.VMEM((chips, rank, share), f32),
            pltpu.VMEM((chips, rank, share), f32),
            pltpu.VMEM((rank, BLOCK), f32),
            pltpu.VMEM((chips, rank, BLOCK), f32),
            pltpu.VMEM((BLOCK, rank), bf16),
            pltpu.VMEM((BLOCK, BLOCK), f32),
            pltpu.VMEM((2, chips, rank, share), f32),
            pltpu.VMEM((chips, rank, share), f32),
            pltpu.VMEM((chips, chips, rank, share), f32),
            pltpu.VMEM((4, rank, hid + 128), jnp.int16),
            pltpu.VMEM((4, rank, hid + 128), jnp.int16),
            pltpu.VMEM((4, rank, hid + 128), jnp.int16),
            pltpu.VMEM((rank, hid), f32),
            pltpu.VMEM((rank, hid), bf16),
            pltpu.VMEM((rank, hid), bf16),
            pltpu.VMEM((rank, 2 * feat), bf16),
            pltpu.VMEM((rank, 2 * feat), bf16),
            pltpu.VMEM((rank, BLOCK), bf16),
            dma((11, 8)),
            dma((11, 8)),
            dma((6, 8)),
            dma((6, 7)),
            dma((6,)),
            dma((6,)),
            dma((6,)),
            dma((4,)),
            dma((11,)),
            dma((11,)),
        ],
        compiler_params=pltpu.CompilerParams(
            collective_id=0, has_side_effects=True, vmem_limit_bytes=62 << 20
        ),
    )(ids, live, store, h, g, w, a_t, b.reshape(rank, wide))
    o_h, o_a, o_b = pl.pallas_call(
        keep,
        out_shape=tuple(jax.ShapeDtypeStruct(o.shape, o.dtype) for o in (o_h, o_a, o_b)),
        in_specs=[far] * 3,
        out_specs=(far,) * 3,
        scratch_shapes=[pltpu.VMEM(o.shape, o.dtype) for o in (o_h, o_a, o_b)] + [dma((3,)), dma((3,))],
        compiler_params=pltpu.CompilerParams(vmem_limit_bytes=62 << 20),
    )(o_h, o_a, o_b)
    return (
        o_h,
        jnp.swapaxes(o_a.reshape(1, rank, hid), 1, 2),
        o_b.reshape(1, rank, wide),
    )


def solution(mesh):
    placed = (
        P("fsdp", "tp"),
        P("tp", "fsdp"),
        P("tp", "fsdp"),
        P("fsdp", "tp", None),
        P("fsdp", None, None),
        P(),
        P(),
        P(),
    )
    return jax.shard_map(
        local,
        mesh=mesh,
        in_specs=placed,
        out_specs=(P("fsdp", "tp"), P("fsdp", "tp", None), P("fsdp", None, None)),
        check_vma=False,
    )
```
